256 devices in a mesh: leaf: 256 (over z, x, y, core).
Axes of the slice: x: 4, y: 4, z: 8, core: 2. Of those that a mesh axis runs over, the one named last changes fastest.
Arguments:
- vectors: float32 [64, 262144], P(None, 'leaf'), may hold values from -6 to 6
- points: float32 [3, 262144], P(None, 'leaf'), may hold values from 0 to 1
- noise: float32 [262144], P('leaf'), may hold values from 0.05 to 1
- bases: float32 [256, 262144], P(None, 'leaf'), may hold values from -0.375 to 0.375
- transfer: float32 [2, 256, 256], replicated, may hold values from -0.25 to 0.25
- proxies: float32 [3, 256], replicated, may hold values from -3.504 to 3.504
- near_src: int32 [1024, 8], P('leaf'), may hold values from 0 to 1023, as said below
- near_count: int32 [1024], P('leaf'), may hold values from 1 to 8
- far_flags: int32 [1792, 3], P('leaf'), may hold values 0 or 1
Outputs:
- product: float32 [64, 262144], P(None, 'leaf')
The draws below stay inside these ranges and needn't reach their ends.
Inputs may be any that keep to these rules, and one draw needn't show every extreme that they name: `near_src`: row n's entries lie within 4 of n; slot 0, and every slot at or past near_count[n], holds n itself.
All inputs are finite; a program needn't handle non-finite values. No bound on the sum of `far_flags` on one device may be relied on, other than what follows from the above.
Results may differ from the reference program's by a relative error of at most 0.0003.
Values sent between devices are 32-bit elements; how exact they have to be, the bound alone decides.
A program may use at most 64 MiB of HBM per device.

```python
import math
import jax
import jax.numpy as jnp
from jax import lax

RANK = 256
RHS = 64
LEAF = 256
NEAR = 8
REACH = 4
LEAVES_DEV = 4
TOTAL_LEAVES = 1024
TOTAL_PTS = 262144
FLAG_ROWS = 1792
N_LEAF = 256


def leaf_counts(key):
    key = jax.random.fold_in(key, 11)
    first_key, second_key, third_key, fourth_key = jax.random.split(key, 4)
    groups = TOTAL_LEAVES // LEAVES_DEV
    device_caps = jax.random.randint(first_key, (groups,), 1, NEAR + 1)
    amounts = jax.random.randint(second_key, (groups, LEAVES_DEV), 1, device_caps[:, None] + 1)
    flat_counts = amounts.reshape(-1)
    positions = jnp.arange(TOTAL_LEAVES, dtype=jnp.int32)
    local_index = positions % LEAVES_DEV
    edge_leaf = (local_index == 0) | (local_index == LEAVES_DEV - 1)
    flat_counts = jnp.where(edge_leaf, jnp.maximum(flat_counts, 2), flat_counts)
    busy_group = jax.random.randint(third_key, (), 0, groups)
    busy_local = jax.random.randint(fourth_key, (), 1, LEAVES_DEV - 2)
    busiest = busy_group * LEAVES_DEV + busy_local
    flat_counts = jnp.where(positions == busiest, NEAR, flat_counts)
    flat_counts = jnp.where(positions == busiest + 1, 1, flat_counts)
    return flat_counts.astype(jnp.int32)


def draw_near_count(key, part):
    return leaf_counts(key)


def draw_near_src(key, part):
    amounts = leaf_counts(key)
    key = jax.random.fold_in(key, 2)
    offsets = jax.random.randint(key, (TOTAL_LEAVES, NEAR), -REACH, REACH + 1)
    readers = jnp.arange(TOTAL_LEAVES, dtype=jnp.int32)[:, None]
    slots = jnp.arange(NEAR, dtype=jnp.int32)[None, :]
    local_index = readers % LEAVES_DEV
    offsets = jnp.where((slots == 1) & (local_index == 0), -REACH, offsets)
    offsets = jnp.where((slots == 1) & (local_index == LEAVES_DEV - 1), REACH, offsets)
    sources = jnp.clip(readers + offsets, 0, TOTAL_LEAVES - 1)
    sources = jnp.where((slots == 0) | (slots >= amounts[:, None]), readers, sources)
    return sources.astype(jnp.int32)


def draw_points(key, part):
    key = jax.random.fold_in(key, 5)
    depth = TOTAL_LEAVES.bit_length() - 1
    leaf_ids = jnp.arange(TOTAL_PTS, dtype=jnp.int32) // LEAF
    cells = [jnp.zeros((TOTAL_PTS,), jnp.int32) for axis_index in range(3)]
    placed = [0, 0, 0]
    for bit_index in range(depth):
        axis_index = (depth - 1 - bit_index) % 3
        bit_value = leaf_ids // 2 ** bit_index % 2
        cells[axis_index] = cells[axis_index] + bit_value * 2 ** placed[axis_index]
        placed[axis_index] = placed[axis_index] + 1
    within = jax.random.uniform(key, (3, TOTAL_PTS), jnp.float32)
    rows = [(cells[axis_index].astype(jnp.float32) + within[axis_index]) / 2.0 ** placed[axis_index] for axis_index in range(3)]
    return jnp.stack(rows).astype(jnp.float32)


def draw_proxies(key, part):
    key = jax.random.fold_in(key, 17)
    order_key, jitter_key = jax.random.split(key)
    order = jax.random.permutation(order_key, RANK).astype(jnp.int32)
    lattice = jnp.stack([order % 8, order // 8 % 8, order // 64]).astype(jnp.float32)
    centred = lattice - jnp.array([3.5, 3.5, 1.5], jnp.float32)[:, None]
    spread = jax.random.uniform(jitter_key, (3, RANK), jnp.float32)
    jitter = 0.004 * (2.0 * spread - 1.0)
    return (centred + jitter).astype(jnp.float32)


def place_ends(entries, key, smallest, high):
    dims = entries.shape
    place = [jax.random.randint(jax.random.fold_in(key, axis), (), 0, dims[axis]) for axis in range(len(dims))]
    entries = entries.at[tuple(place)].set(smallest)
    longest = dims.index(max(dims))
    place[longest] = (place[longest] + 1) % dims[longest]
    return entries.at[tuple(place)].set(high)


def levels(rng, extent, cuts, least, largest):
    loudness, own = 1.0, jax.random.fold_in(rng, 6)
    for axis_at, shards_of in cuts:
        steps = jnp.exp(jax.random.uniform(jax.random.fold_in(own, axis_at), (shards_of,), jnp.float32, least / len(cuts), largest / len(cuts)))
        loudness = loudness * jnp.repeat(steps, extent[axis_at] // shards_of).reshape([-1 if axis == axis_at else 1 for axis in range(len(extent))])
    return loudness


def bell_draw(stream_key, shape, scale, bound, shards=(), held_as=jnp.bfloat16):
    values = jax.random.normal(stream_key, shape, jnp.float32) * scale
    if len(shards) > 0:
        values = levels(stream_key, shape, shards, -0.22, 0.18) * values
    return jnp.clip(values, min=-bound, max=bound).astype(held_as)


def setup_inputs(seed: int = 0) -> dict:
    arg_keys = jax.random.split(jax.random.key(seed), 10)
    return {
        "vectors": bell_draw(arg_keys[0], (RHS, TOTAL_PTS), 1.0, 6.0, ((1, 256),), jnp.float32),
        "points": draw_points(jax.random.fold_in(arg_keys[9], 71), 0),
        "noise": jnp.clip(jnp.exp(math.log(1.0) - 2.9957323 * jax.random.uniform(arg_keys[2], (TOTAL_PTS,), jnp.float32) ** levels(arg_keys[2], (TOTAL_PTS,), ((0, 256),), -0.2, 0.2)), 0.05, 1.0),
        "bases": bell_draw(arg_keys[3], (RANK, TOTAL_PTS), LEAF ** -0.5, 0.375, ((1, 256),), jnp.float32),
        "transfer": bell_draw(arg_keys[4], (2, RANK, RANK), (2 * RANK) ** -0.5, 0.25, (), jnp.float32),
        "proxies": draw_proxies(jax.random.fold_in(arg_keys[9], 71), 0),
        "near_src": draw_near_src(jax.random.fold_in(arg_keys[9], 71), 0),
        "near_count": draw_near_count(jax.random.fold_in(arg_keys[9], 71), 0),
        "far_flags": place_ends((jax.random.randint(arg_keys[8], (FLAG_ROWS, 3), 0, 4) < 3).astype(jnp.int32), jax.random.fold_in(arg_keys[8], 1), 0, 1),
    }


SHORT_SCALE = 0.02
LONG_SCALE = 1.0
ROOT_THREE = 1.7320508075688772
HIGHEST = lax.Precision.HIGHEST

def matern(squared):
    distance = jnp.sqrt(squared)
    short_arg = ROOT_THREE / SHORT_SCALE * distance
    long_arg = ROOT_THREE / LONG_SCALE * distance
    return 0.5 * (1.0 + short_arg) * jnp.exp(-short_arg) + 0.5 * (1.0 + long_arg) * jnp.exp(-long_arg)

def level_kernels(proxies, level_index, top_level):
    box_side = 2.0 ** ((level_index - top_level) / 3.0)
    differences = box_side * (proxies[:, :, None] - proxies[:, None, :])
    direction = (jnp.arange(3) == level_index % 3).astype(jnp.float32)[:, None, None]
    kernels = []
    for offset in (2.0, 3.0):
        displaced = differences - offset * box_side * direction
        kernels.append(matern(lax.optimization_barrier(jnp.sum(displaced * displaced, axis=0))))
    return (kernels[0], kernels[1])

def near_term(reader_points, source_points, source_vecs, active):
    differences = reader_points[:, :, :, None] - source_points[:, :, None, :]
    kernel = matern(lax.optimization_barrier(jnp.sum(differences * differences, axis=0)))
    scale = source_vecs.shape[2] ** (-0.5)
    contrib = jnp.einsum('iab,sib->sia', kernel, source_vecs, precision=HIGHEST)
    return contrib * (scale * active)[None, :, None]

def level_field(extended, weights, kernel_two, kernel_three):
    nodes = extended.shape[0] - 4
    minus_two = extended[0:nodes]
    plus_two = extended[4:nodes + 4]
    plus_three = extended[5:nodes + 5:2]
    minus_three = extended[0:nodes:2]
    first = jnp.einsum('nsb,ba->nsa', minus_two, kernel_two, precision=HIGHEST)
    second = jnp.einsum('nsb,ab->nsa', plus_two, kernel_two, precision=HIGHEST)
    even_part = jnp.einsum('nsb,ab->nsa', plus_three, kernel_three, precision=HIGHEST)
    odd_part = jnp.einsum('nsb,ba->nsa', minus_three, kernel_three, precision=HIGHEST)
    third = jnp.stack([even_part, odd_part], axis=1).reshape(minus_two.shape)
    scale = minus_two.shape[-1] ** (-0.5)
    return scale * (weights[:, 0, None, None] * first + weights[:, 1, None, None] * second + weights[:, 2, None, None] * third)

def parents_of(children, transfer):
    left_part = jnp.einsum('nsr,rq->nsq', children[0::2], transfer[0], precision=HIGHEST)
    right_part = jnp.einsum('nsr,rq->nsq', children[1::2], transfer[1], precision=HIGHEST)
    return left_part + right_part

def children_of(parents, fields, transfer):
    even_nodes = fields[0::2] + jnp.einsum('nsq,rq->nsr', parents, transfer[0], precision=HIGHEST)
    odd_nodes = fields[1::2] + jnp.einsum('nsq,rq->nsr', parents, transfer[1], precision=HIGHEST)
    return jnp.stack([even_nodes, odd_nodes], axis=1).reshape(fields.shape)

def reference(vectors, points, noise, bases, transfer, proxies, near_src, near_count, far_flags):
    rank_size = bases.shape[0]
    rhs_count = vectors.shape[0]
    depth = N_LEAF.bit_length() - 1
    local_levels = LEAVES_DEV.bit_length() - 1
    top_level = local_levels + depth
    leaf_vecs = vectors.reshape(rhs_count, TOTAL_LEAVES, LEAF)
    leaf_bases = bases.reshape(rank_size, TOTAL_LEAVES, LEAF)
    leaf_points = points.reshape(3, TOTAL_LEAVES, LEAF)

    def group_near(group_index):
        first_leaf = group_index * LEAVES_DEV
        readers = lax.dynamic_slice_in_dim(leaf_points, first_leaf, LEAVES_DEV, 1)
        lists = lax.dynamic_slice_in_dim(near_src, first_leaf, LEAVES_DEV, 0)
        amounts = lax.dynamic_slice_in_dim(near_count, first_leaf, LEAVES_DEV, 0)
        total = jnp.zeros((rhs_count, LEAVES_DEV, LEAF), jnp.float32)
        for slot_index in range(NEAR):
            sources = lists[:, slot_index]
            active = (slot_index < amounts).astype(jnp.float32)
            source_points = jnp.take(leaf_points, sources, axis=1)
            source_vecs = jnp.take(leaf_vecs, sources, axis=1)
            total = total + near_term(readers, source_points, source_vecs, active)
        return total
    blocks = lax.map(group_near, jnp.arange(N_LEAF, dtype=jnp.int32))
    near_field = blocks.transpose(1, 0, 2, 3).reshape(rhs_count, TOTAL_LEAVES, LEAF)
    coefs = [jnp.einsum('sip,rip->isr', leaf_vecs, leaf_bases, precision=HIGHEST)]
    for level_index in range(top_level):
        coefs.append(parents_of(coefs[-1], transfer))
    flag_table = far_flags.astype(jnp.float32).reshape(N_LEAF, 2 * LEAVES_DEV - 1, 3)
    fields = []
    first_row = 0
    for level_index in range(top_level):
        nodes = TOTAL_LEAVES >> level_index
        if level_index <= local_levels:
            per_device = LEAVES_DEV >> level_index
            weights = flag_table[:, first_row:first_row + per_device].reshape(nodes, 3)
            first_row = first_row + per_device
        else:
            weights = jnp.ones((nodes, 3), jnp.float32)
        kernel_two, kernel_three = level_kernels(proxies, level_index, top_level)
        padded = jnp.pad(coefs[level_index], ((2, 2), (0, 0), (0, 0)))
        fields.append(level_field(padded, weights, kernel_two, kernel_three))
    downward = jnp.zeros_like(coefs[top_level])
    for level_index in range(top_level - 1, -1, -1):
        downward = children_of(downward, fields[level_index], transfer)
    far_field = jnp.einsum('isr,rip->sip', downward, leaf_bases, precision=HIGHEST)
    result = noise.reshape(1, TOTAL_LEAVES, LEAF) * leaf_vecs + far_field + near_field
    return result.reshape(rhs_count, TOTAL_LEAVES * LEAF)
```

```python
import functools
import math

import jax
import jax.numpy as jnp
from jax import lax
from jax.experimental import pallas as pl
from jax.experimental.pallas import tpu as pltpu
from jax.sharding import PartitionSpec as P

SHORT_SCALE = 0.02
LONG_SCALE = 1.0
ROOT_THREE = 1.7320508075688772
LOG2_E = 1.4426950408889634

F32 = jnp.float32
BF16 = jnp.bfloat16
MESH = pl.DeviceIdType.MESH

LEAVES = 4
LEAF = 256
RANK = 256
RHS = 64
ROWS = 2
PLANE = 32
PLANES = 8
DEVICES = PLANE * PLANES
TOP = 10
HALO = 3
CHUNK = 32

NORMAL = (((1,), (0,)), ((), ()))
TRANSPOSED = (((1,), (1,)), ((), ()))

PLANE_LEVELS = (2, 3, 4, 5, 6)

SEM_A, SEM_TOP, SEM_B = 0, 1, 2
SEM_VEC, SEM_PTS, SEM_RIM0, SEM_RIM1, SEM_EDGE = 3, 5, 7, 9, 11
SEMS = SEM_EDGE + 2 * len(PLANE_LEVELS)


def nodes_at(level):
    return PLANE >> (level - 2)


def reversed_bits(value, count):
    result = 0
    for bit in range(count):
        result = result * 2 + (value >> bit & 1)
    return result


def halves(x):
    head = x.astype(BF16).astype(F32)
    return jnp.concatenate([head, x - head], axis=0).astype(BF16)


def head_and_rest(x):
    head = x.astype(BF16)
    return head, (x - head.astype(F32)).astype(BF16)


def mul(stacked, w_head, w_rest, dims=NORMAL):
    rows = stacked.shape[0] // 2
    if rows % 16 == 0:
        first = lax.dot_general(stacked, w_head, dims, preferred_element_type=F32)
        second = lax.dot_general(stacked[:rows], w_rest, dims, preferred_element_type=F32)
        return first[:rows] + first[rows:] + second
    both = lax.dot_general(stacked, w_head, dims, preferred_element_type=F32)
    both = both + lax.dot_general(stacked, w_rest, dims, preferred_element_type=F32)
    return both[:rows] + both[rows:]


def stack(first, second, rows):
    if rows % 8 == 0:
        return jnp.concatenate([first[:rows], second[:rows]], axis=0)
    place = lax.broadcasted_iota(jnp.int32, first.shape, 0)
    return jnp.where(place < rows, first, pltpu.roll(second, rows, 0))


def second_half(x, rows):
    if rows % 8 == 0:
        return x[rows:]
    return pltpu.roll(x, x.shape[0] - rows, 0)


def kernel(
    vec,
    pts,
    noise,
    bases,
    transfer,
    prox,
    src,
    cnt,
    flags,
    out,
    vhl,
    bh,
    bl,
    th,
    tl,
    vside,
    ppad,
    pside,
    cols,
    kh,
    kl,
    ch,
    cl,
    near,
    ex0,
    ex1,
    f0,
    f1,
    sa,
    sb,
    rb,
    s7,
    e2,
    e3,
    e4,
    e5,
    e6,
    top7,
    top8,
    gm,
    gp,
    ge,
    go,
    gf,
    g2,
    fs,
    send,
    recv,
):
    edge_of = {2: e2, 3: e3, 4: e4, 5: e5, 6: e6}
    me = lax.axis_index("leaf")
    z, j = me // PLANE, me % PLANE
    left = (me + DEVICES - 1) % DEVICES
    right = (me + 1) % DEVICES
    below = (me + DEVICES - PLANE) % DEVICES
    above = (me + PLANE) % DEVICES

    barrier = pltpu.get_barrier_semaphore()

    def greet(device):
        pl.semaphore_signal(barrier, inc=1, device_id=(device,), device_id_type=MESH)

    @pl.loop(1, PLANE)
    def _(step):
        greet(z * PLANE + (j + step) % PLANE)

    @pl.loop(1, PLANES)
    def _(step):
        greet((z + step) % PLANES * PLANE + j)

    greet(left)
    greet(right)

    def copy(source, target, sem, device):
        return pltpu.make_async_remote_copy(
            src_ref=source,
            dst_ref=target,
            send_sem=send.at[sem],
            recv_sem=recv.at[sem],
            device_id=(device,),
            device_id_type=MESH,
        )

    head, rest = head_and_rest(transfer[...].reshape(2 * RANK, RANK))
    th[...] = head
    tl[...] = rest
    coef0 = []
    for leaf in range(LEAVES):
        lanes = slice(leaf * LEAF, (leaf + 1) * LEAF)
        head, rest = head_and_rest(bases[:, lanes])
        bh[:, lanes] = head
        bl[:, lanes] = rest
        pair = halves(vec[:, lanes])
        vhl[4 + leaf] = pair
        value = mul(pair, head, rest, TRANSPOSED)
        ex0[2 + leaf] = value
        coef0.append(value)

    def parents(children):
        return mul(halves(children), th[...], tl[...])

    pair_rows = [jnp.concatenate([coef0[2 * n], coef0[2 * n + 1]], axis=1) for n in range(2)]
    coef1 = parents(jnp.concatenate(pair_rows, axis=0))
    ex1[2] = coef1[:RHS]
    ex1[3] = coef1[RHS:]
    coef2 = parents(jnp.concatenate([coef1[:RHS], coef1[RHS:]], axis=1))

    lane = lax.broadcasted_iota(jnp.int32, (ROWS, 128), 1)
    root_flags = jnp.zeros((ROWS, 128), F32)
    for which in range(3):
        root_flags = jnp.where(lane == which, flags[6, which].astype(F32), root_flags)
    g2[...] = coef2
    for i in range(PLANE):
        sa[i, :, 0:RANK] = g2[ROWS * i : ROWS * (i + 1), :]
        sa[i, :, RANK:] = root_flags

    pl.semaphore_wait(barrier, PLANE - 1 + PLANES - 1 + 2)

    @pl.loop(1, PLANE)
    def _(step):
        other = (j + step) % PLANE
        copy(sa.at[other], e2.at[HALO + j], SEM_A, z * PLANE + other).start()

    e2[HALO + j] = sa[j]

    ppad[...] = jnp.zeros_like(ppad)
    ppad[0:3, :] = pts[...]
    side_copies = [
        copy(ppad, pside.at[0], SEM_PTS, right),
        copy(ppad, pside.at[1], SEM_PTS + 1, left),
        copy(vec, vside.at[0], SEM_VEC, right),
        copy(vec, vside.at[1], SEM_VEC + 1, left),
        copy(ex0.at[pl.ds(4, 2)], ex0.at[pl.ds(0, 2)], SEM_RIM0, right),
        copy(ex0.at[pl.ds(2, 2)], ex0.at[pl.ds(6, 2)], SEM_RIM0 + 1, left),
        copy(ex1.at[pl.ds(2, 2)], ex1.at[pl.ds(0, 2)], SEM_RIM1, right),
        copy(ex1.at[pl.ds(2, 2)], ex1.at[pl.ds(4, 2)], SEM_RIM1 + 1, left),
    ]
    for item in side_copies:
        item.start()

    prox_rows = prox[...]
    prox_cols = jnp.concatenate([prox_rows, jnp.zeros((5, RANK), F32)], axis=0).T
    gf[...] = prox_cols

    for axis in range(3):
        side = 2.0 ** ((axis - TOP) / 3.0)
        for place, offset in enumerate((2.0, 3.0)):

            @pl.loop(0, RANK // CHUNK)
            def _(step):
                rows = pl.ds(step * CHUNK, CHUNK)
                squared = None
                for c in range(3):
                    column = gf[rows, c : c + 1]
                    if c == axis:
                        column = column - offset
                    delta = column - prox_rows[c : c + 1, :]
                    squared = delta * delta if squared is None else squared + delta * delta
                distance = squared * lax.rsqrt(jnp.maximum(squared, 1e-30))
                u = distance * (ROOT_THREE / SHORT_SCALE * side)
                v = distance * (ROOT_THREE / LONG_SCALE * side)
                eu = jnp.exp2(u * -LOG2_E)
                ev = jnp.exp2(v * -LOG2_E)
                for third in range(3):
                    value = (1.0 + u) * eu + (1.0 + v) * ev
                    head, rest = head_and_rest(value)
                    at = 2 * (axis + 3 * third) + place
                    ch[at, rows, :] = head
                    cl[at, rows, :] = rest
                    if third < 2:
                        u, v, eu, ev = u + u, v + v, eu * eu, ev * ev

    def field(level, minus, plus, even, odd, rows):
        two, three = 2 * level, 2 * level + 1
        first = mul(halves(minus), ch[two], cl[two])
        second = mul(halves(plus), ch[two], cl[two], TRANSPOSED)
        even_part = mul(halves(even), ch[three], cl[three], TRANSPOSED)
        odd_part = mul(halves(odd), ch[three], cl[three])
        if rows is None:
            return first, second, even_part, odd_part
        return (first + second + stack(even_part, odd_part, rows)) * (1.0 / 32.0)

    gm[...] = jnp.zeros_like(gm)
    gp[...] = jnp.zeros_like(gp)
    ge[...] = jnp.zeros_like(ge)
    go[...] = jnp.zeros_like(go)

    def columns_of(window, points):
        cols[window] = points.T

    def evaluate(reader, window, slot):
        reader_rows = ppad[:, pl.ds(pl.multiple_of(reader * LEAF, LEAF), LEAF)]

        @pl.loop(0, LEAF // CHUNK)
        def _(step):
            rows = pl.ds(step * CHUNK, CHUNK)
            squared = None
            for c in range(3):
                delta = cols[window, rows, c : c + 1] - reader_rows[c : c + 1, :]
                squared = delta * delta if squared is None else squared + delta * delta
            distance = squared * lax.rsqrt(jnp.maximum(squared, 1e-30))
            u = distance * (ROOT_THREE / SHORT_SCALE)
            v = distance * (ROOT_THREE / LONG_SCALE)
            value = (1.0 + u) * jnp.exp2(u * -LOG2_E) + (1.0 + v) * jnp.exp2(v * -LOG2_E)
            head, rest = head_and_rest(value)
            kh[slot, rows, :] = head
            kl[slot, rows, :] = rest

    def amount(reader, window):
        target = me * LEAVES + window - 4
        total = jnp.float32(0.0)
        for slot in range(8):
            hit = jnp.logical_and(slot < cnt[reader], src[reader, slot] == target)
            total = total + jnp.where(hit, 1.0, 0.0)
        return total

    def gather_near(reader, window, slot, dims):
        near[reader] += amount(reader, window) * mul(vhl[window], kh[slot], kl[slot], dims)

    near[...] = jnp.zeros_like(near)
    for leaf in range(LEAVES):
        columns_of(4 + leaf, ppad[:, leaf * LEAF : (leaf + 1) * LEAF])

    @pl.loop(0, LEAVES)
    def _(leaf):
        evaluate(leaf, 4 + leaf, 0)
        gather_near(leaf, 4 + leaf, 0, NORMAL)

    copy(sa.at[pl.ds(0, PLANE - 1)], e2.at[pl.ds(HALO, PLANE - 1)], SEM_A, left).wait_recv()
    edge_copies = []

    def send_edges(level):
        ref, nodes = edge_of[level], nodes_at(level)
        width = min(HALO, nodes)
        at = SEM_EDGE + 2 * (level - 2)
        for item in (
            copy(
                ref.at[pl.ds(HALO + nodes - width, width)],
                ref.at[pl.ds(HALO - width, width)],
                at,
                above,
            ),
            copy(ref.at[pl.ds(HALO, width)], ref.at[pl.ds(HALO + nodes, width)], at + 1, below),
        ):
            item.start()
            edge_copies.append(item)

    send_edges(2)
    for p in range(PLANE):
        g2[ROWS * p : ROWS * (p + 1), :] = e2[HALO + reversed_bits(p, 5), :, 0:RANK]
    current = g2[...]
    for level in (3, 4, 5, 6, 7):
        rows = ROWS * nodes_at(level)
        both = jnp.concatenate([current[: max(rows, 8)], second_half(current, rows)], axis=1)
        current = parents(both)
        if level < 7:
            count = 7 - level
            for p in range(nodes_at(level)):
                edge_of[level][HALO + reversed_bits(p, count)] = current[ROWS * p : ROWS * (p + 1)]
            send_edges(level)
    s7[...] = current[0:ROWS]

    @pl.loop(1, PLANES)
    def _(step):
        other = (z + step) % PLANES
        copy(s7, top7.at[HALO + z], SEM_TOP, other * PLANE + j).start()

    top7[HALO + z] = s7[...]
    top7[0:HALO] = jnp.zeros((HALO, ROWS, RANK), F32)
    top7[HALO + PLANES :] = jnp.zeros((HALO, ROWS, RANK), F32)
    top8[...] = jnp.zeros_like(top8)

    inside_below = jnp.where(z > 0, 1.0, 0.0)
    inside_above = jnp.where(z < PLANES - 1, 1.0, 0.0)
    for item in edge_copies:
        item.wait_recv()

    def plane_field(level):
        ref, nodes = edge_of[level], nodes_at(level)
        count = 7 - level

        def at(node):
            value = ref[HALO + node, :, 0:RANK]
            if node < 0:
                value = value * inside_below
            if node >= nodes:
                value = value * inside_above
            return value

        for p in range(nodes):
            node = reversed_bits(p, count)
            rows = slice(ROWS * p, ROWS * (p + 1))
            gm[rows, :] = at(node - 2)
            gp[rows, :] = at(node + 2)
            if p < nodes // 2:
                ge[rows, :] = at(node + 3)
            else:
                half = p - nodes // 2
                go[ROWS * half : ROWS * (half + 1), :] = at(node - 3)
            if level == 2:
                gf[rows, :] = ref[HALO + node, :, RANK : RANK + 8]
        size = max(ROWS * nodes, 8)
        half_size = max(ROWS * nodes // 2, 8)
        minus, plus = gm[0:size, :], gp[0:size, :]
        even, odd = ge[0:half_size, :], go[0:half_size, :]
        if level == 2:
            weights = gf[0:size, :]
            minus = minus * weights[:, 0:1]
            plus = plus * weights[:, 1:2]
            even = even * weights[:half_size, 2:3]
            odd = odd * weights[half_size:, 2:3]
        fs[level - 2, 0:size, :] = field(level, minus, plus, even, odd, ROWS * nodes // 2)

    for level in PLANE_LEVELS:
        plane_field(level)

    copy(
        top7.at[pl.ds(HALO, PLANES - 1)], top7.at[pl.ds(HALO, PLANES - 1)], SEM_TOP, left
    ).wait_recv()
    for p in range(PLANES):
        g2[ROWS * p : ROWS * (p + 1), :] = top7[HALO + reversed_bits(p, 3)]
    coef8 = parents(jnp.concatenate([g2[0:8, :], g2[8:16, :]], axis=1))
    for p in range(4):
        top8[HALO + reversed_bits(p, 2)] = coef8[ROWS * p : ROWS * (p + 1)]

    def own_field(level, ref, node):
        parity = node % 2
        gm[0:ROWS, :] = ref[HALO + node - 2]
        gp[0:ROWS, :] = ref[HALO + node + 2]
        ge[0:ROWS, :] = ref[jnp.where(parity == 0, HALO + node + 3, HALO + node - 3)]
        third = ge[0:8, :]
        first, second, even, odd = field(level, gm[0:8, :], gp[0:8, :], third, third, None)
        return (first + second + jnp.where(parity == 0, even, odd)) * (1.0 / 32.0)

    def children(parent):
        return mul(halves(parent), th[...], tl[...], TRANSPOSED)

    field7 = own_field(7, top7, z)
    down = own_field(8, top8, z // 2)
    both = children(down)
    down = field7 + jnp.where(z % 2 == 0, both[:, :RANK], both[:, RANK:])
    for level in (6, 5, 4, 3, 2):
        size = max(ROWS * nodes_at(level), 8)
        both = children(down)
        rows = ROWS * nodes_at(level) // 2
        down = fs[level - 2, 0:size, :] + stack(both[:, :RANK], both[:, RANK:], rows)
    for p in range(PLANE):
        sb[reversed_bits(p, 5)] = down[ROWS * p : ROWS * (p + 1)]

    @pl.loop(1, PLANE)
    def _(step):
        other = (j + step) % PLANE
        copy(sb.at[other], rb.at[j], SEM_B, z * PLANE + other).start()

    rb[j] = sb[j]

    for item in side_copies:
        item.wait_recv()
    has_left = jnp.where(me > 0, 1.0, 0.0)
    has_right = jnp.where(me < DEVICES - 1, 1.0, 0.0)

    def local_field(level, ref, nodes, first_row, target):
        def at(node, which, reader):
            weight = flags[first_row + reader, which].astype(F32)
            if node < 0:
                weight = weight * has_left
            if node >= nodes:
                weight = weight * has_right
            return ref[2 + node] * weight

        order = list(range(0, nodes, 2)) + list(range(1, nodes, 2))
        minus = jnp.concatenate([at(n - 2, 0, n) for n in order], axis=0)
        plus = jnp.concatenate([at(n + 2, 1, n) for n in order], axis=0)
        even = jnp.concatenate([at(n + 3, 2, n) for n in range(0, nodes, 2)], axis=0)
        odd = jnp.concatenate([at(n - 3, 2, n) for n in range(1, nodes, 2)], axis=0)
        value = field(level, minus, plus, even, odd, RHS * nodes // 2)
        for place, n in enumerate(order):
            target[n] = value[RHS * place : RHS * (place + 1)]

    local_field(0, ex0, LEAVES, 0, f0)
    local_field(1, ex1, LEAVES // 2, LEAVES, f1)

    for leaf in range(LEAVES):
        lanes = slice(leaf * LEAF, (leaf + 1) * LEAF)
        vhl[leaf] = halves(vside[0, :, lanes])
        vhl[8 + leaf] = halves(vside[1, :, lanes])
        columns_of(leaf, pside[0, :, lanes])
        columns_of(8 + leaf, pside[1, :, lanes])

    for first in range(LEAVES):
        for second in range(first + 1, LEAVES):
            evaluate(first, 4 + second, 0)
            gather_near(first, 4 + second, 0, NORMAL)
            gather_near(second, 4 + first, 0, TRANSPOSED)

    @pl.loop(0, 5 * LEAVES)
    def _(index):
        reader = index // 5
        step = index % 5
        window = reader + step + jnp.where(step < 4 - reader, 0, 4)
        evaluate(reader, window, 0)
        gather_near(reader, window, 0, NORMAL)

    copy(sb.at[pl.ds(0, PLANE - 1)], rb.at[pl.ds(0, PLANE - 1)], SEM_B, left).wait_recv()
    for i in range(PLANE):
        g2[ROWS * i : ROWS * (i + 1), :] = rb[i]
    both = children(g2[...])
    down1 = jnp.concatenate([f1[0] + both[:, :RANK], f1[1] + both[:, RANK:]], axis=0)
    both = children(down1)
    for leaf in range(LEAVES):
        lanes = slice(leaf * LEAF, (leaf + 1) * LEAF)
        part = both[RHS * (leaf // 2) : RHS * (leaf // 2 + 1)]
        part = part[:, RANK * (leaf % 2) : RANK * (leaf % 2 + 1)]
        far = mul(halves(f0[leaf] + part), bh[:, lanes], bl[:, lanes])
        own = noise[:, lanes] * vec[:, lanes]
        out[:, lanes] = own + far + near[leaf] * (1.0 / 32.0)

    copy(sa.at[pl.ds(0, PLANE - 1)], e2.at[pl.ds(HALO, PLANE - 1)], SEM_A, left).wait_send()
    copy(sb.at[pl.ds(0, PLANE - 1)], rb.at[pl.ds(0, PLANE - 1)], SEM_B, left).wait_send()
    copy(
        top7.at[pl.ds(HALO, PLANES - 1)], top7.at[pl.ds(HALO, PLANES - 1)], SEM_TOP, left
    ).wait_send()
    for item in side_copies + edge_copies:
        item.wait_send()


def on_device(vectors, points, noise, bases, transfer, proxies, near_src, near_count, far_flags):
    vmem = pl.BlockSpec(memory_space=pltpu.VMEM)
    smem = pl.BlockSpec(memory_space=pltpu.SMEM)
    width = RANK + 128

    def buffer(*shape, dtype=F32):
        return pltpu.VMEM(shape, dtype)

    scratch = [
        buffer(12, 2 * RHS, LEAF, dtype=BF16),
        buffer(RANK, LEAVES * LEAF, dtype=BF16),
        buffer(RANK, LEAVES * LEAF, dtype=BF16),
        buffer(2 * RANK, RANK, dtype=BF16),
        buffer(2 * RANK, RANK, dtype=BF16),
        buffer(2, RHS, LEAVES * LEAF),
        buffer(8, LEAVES * LEAF),
        buffer(2, 8, LEAVES * LEAF),
        buffer(12, LEAF, 8),
        buffer(2, LEAF, LEAF, dtype=BF16),
        buffer(2, LEAF, LEAF, dtype=BF16),
        buffer(18, RANK, RANK, dtype=BF16),
        buffer(18, RANK, RANK, dtype=BF16),
        buffer(LEAVES, RHS, LEAF),
        buffer(LEAVES + 4, RHS, RANK),
        buffer(LEAVES // 2 + 4, RHS, RANK),
        buffer(LEAVES, RHS, RANK),
        buffer(LEAVES // 2, RHS, RANK),
        buffer(PLANE, ROWS, width),
        buffer(PLANE, ROWS, RANK),
        buffer(PLANE, ROWS, RANK),
        buffer(ROWS, RANK),
        buffer(PLANE + 2 * HALO, ROWS, width),
    ]
    for level in PLANE_LEVELS[1:]:
        scratch.append(buffer(nodes_at(level) + 2 * HALO, ROWS, RANK))
    scratch += [
        buffer(PLANES + 2 * HALO, ROWS, RANK),
        buffer(4 + 2 * HALO, ROWS, RANK),
        buffer(RHS, RANK),
        buffer(RHS, RANK),
        buffer(RHS, RANK),
        buffer(RHS, RANK),
        buffer(RANK, 8),
        buffer(RHS, RANK),
        buffer(len(PLANE_LEVELS), RHS, RANK),
        pltpu.SemaphoreType.DMA((SEMS,)),
        pltpu.SemaphoreType.DMA((SEMS,)),
    ]
    return pl.pallas_call(
        kernel,
        out_shape=jax.ShapeDtypeStruct(vectors.shape, F32),
        in_specs=[vmem] * 6 + [smem] * 3,
        out_specs=vmem,
        scratch_shapes=scratch,
        compiler_params=pltpu.CompilerParams(
            collective_id=0, has_side_effects=True, vmem_limit_bytes=48 * 2**20
        ),
        cost_estimate=pl.CostEstimate(
            flops=3 * 10**9, bytes_accessed=3 * 10**6, transcendentals=10**7
        ),
    )(
        vectors,
        points,
        noise.reshape(1, -1),
        bases,
        transfer,
        proxies,
        near_src,
        near_count,
        far_flags,
    )


def solution(mesh):
    in_specs = (
        P(None, "leaf"),
        P(None, "leaf"),
        P("leaf"),
        P(None, "leaf"),
        P(),
        P(),
        P("leaf", None),
        P("leaf"),
        P("leaf", None),
    )
    return jax.shard_map(
        on_device, mesh=mesh, in_specs=in_specs, out_specs=P(None, "leaf"), check_vma=False
    )
```

```python
import functools
import math

import jax
import jax.numpy as jnp
from jax import lax
from jax.experimental import pallas as pl
from jax.experimental.pallas import tpu as pltpu
from jax.sharding import PartitionSpec as P

SHORT_SCALE = 0.02
LONG_SCALE = 1.0
ROOT_THREE = 1.7320508075688772
LOG2_E = 1.4426950408889634

F32 = jnp.float32
BF16 = jnp.bfloat16
MESH = pl.DeviceIdType.MESH

LEAVES = 4
LEAF = 256
RANK = 256
RHS = 64
ROWS = 2
PLANE = 32
PLANES = 8
DEVICES = PLANE * PLANES
TOP = 10
HALO = 3
CHUNK = 32

NORMAL = (((1,), (0,)), ((), ()))
TRANSPOSED = (((1,), (1,)), ((), ()))

PLANE_LEVELS = (2, 3, 4, 5, 6)

SEM_A, SEM_TOP, SEM_B = 0, 1, 2
SEM_VEC, SEM_PTS, SEM_RIM0, SEM_RIM1, SEM_EDGE = 3, 5, 7, 9, 11
SEMS = SEM_EDGE + 2 * len(PLANE_LEVELS)


def nodes_at(level):
    return PLANE >> (level - 2)


def reversed_bits(value, count):
    result = 0
    for bit in range(count):
        result = result * 2 + (value >> bit & 1)
    return result


def halves(x):
    head = x.astype(BF16).astype(F32)
    return jnp.concatenate([head, x - head], axis=0).astype(BF16)


def head_and_rest(x):
    head = x.astype(BF16)
    return head, (x - head.astype(F32)).astype(BF16)


def mul(stacked, w_head, w_rest, dims=NORMAL):
    rows = stacked.shape[0] // 2
    if rows % 16 == 0:
        first = lax.dot_general(stacked, w_head, dims, preferred_element_type=F32)
        second = lax.dot_general(stacked[:rows], w_rest, dims, preferred_element_type=F32)
        return first[:rows] + first[rows:] + second
    both = lax.dot_general(stacked, w_head, dims, preferred_element_type=F32)
    both = both + lax.dot_general(stacked, w_rest, dims, preferred_element_type=F32)
    return both[:rows] + both[rows:]


def stack(first, second, rows):
    if rows % 8 == 0:
        return jnp.concatenate([first[:rows], second[:rows]], axis=0)
    place = lax.broadcasted_iota(jnp.int32, first.shape, 0)
    return jnp.where(place < rows, first, pltpu.roll(second, rows, 0))


def second_half(x, rows):
    if rows % 8 == 0:
        return x[rows:]
    return pltpu.roll(x, x.shape[0] - rows, 0)


def kernel(
    vec_in,
    pts_in,
    noise_in,
    bases_in,
    transfer_in,
    prox_in,
    src_in,
    cnt_in,
    flags_in,
    out,
    vec,
    pts,
    noise,
    bases,
    transfer,
    prox,
    src,
    cnt,
    flags,
    vhl,
    bh,
    bl,
    th,
    tl,
    vside,
    ppad,
    pside,
    cols,
    kh,
    kl,
    ch,
    cl,
    near,
    ex0,
    ex1,
    f0,
    f1,
    sa,
    sb,
    rb,
    s7,
    e2,
    e3,
    e4,
    e5,
    e6,
    top7,
    top8,
    gm,
    gp,
    ge,
    go,
    gf,
    g2,
    fs,
    load,
    send,
    recv,
):
    loads = [
        pltpu.make_async_copy(source, target, load.at[place])
        for place, (source, target) in enumerate(
            (
                (vec_in, vec),
                (bases_in, bases),
                (transfer_in, transfer),
                (pts_in, pts),
                (prox_in, prox),
                (noise_in, noise),
                (src_in, src),
                (cnt_in, cnt),
                (flags_in, flags),
            )
        )
    ]
    for item in loads:
        item.start()
    edge_of = {2: e2, 3: e3, 4: e4, 5: e5, 6: e6}
    me = lax.axis_index("leaf")
    z, j = me // PLANE, me % PLANE
    left = (me + DEVICES - 1) % DEVICES
    right = (me + 1) % DEVICES
    below = (me + DEVICES - PLANE) % DEVICES
    above = (me + PLANE) % DEVICES

    barrier = pltpu.get_barrier_semaphore()

    def greet(device):
        pl.semaphore_signal(barrier, inc=1, device_id=(device,), device_id_type=MESH)

    @pl.loop(1, PLANE)
    def _(step):
        greet(z * PLANE + (j + step) % PLANE)

    @pl.loop(1, PLANES)
    def _(step):
        greet((z + step) % PLANES * PLANE + j)

    greet(left)
    greet(right)

    def copy(source, target, sem, device):
        return pltpu.make_async_remote_copy(
            src_ref=source,
            dst_ref=target,
            send_sem=send.at[sem],
            recv_sem=recv.at[sem],
            device_id=(device,),
            device_id_type=MESH,
        )

    for item in loads:
        item.wait()
    head, rest = head_and_rest(transfer[...].reshape(2 * RANK, RANK))
    th[...] = head
    tl[...] = rest
    coef0 = []
    for leaf in range(LEAVES):
        lanes = slice(leaf * LEAF, (leaf + 1) * LEAF)
        head, rest = head_and_rest(bases[:, lanes])
        bh[:, lanes] = head
        bl[:, lanes] = rest
        pair = halves(vec[:, lanes])
        vhl[4 + leaf] = pair
        value = mul(pair, head, rest, TRANSPOSED)
        ex0[2 + leaf] = value
        coef0.append(value)

    def parents(children):
        return mul(halves(children), th[...], tl[...])

    pair_rows = [jnp.concatenate([coef0[2 * n], coef0[2 * n + 1]], axis=1) for n in range(2)]
    coef1 = parents(jnp.concatenate(pair_rows, axis=0))
    ex1[2] = coef1[:RHS]
    ex1[3] = coef1[RHS:]
    coef2 = parents(jnp.concatenate([coef1[:RHS], coef1[RHS:]], axis=1))

    lane = lax.broadcasted_iota(jnp.int32, (ROWS, 128), 1)
    root_flags = jnp.zeros((ROWS, 128), F32)
    for which in range(3):
        root_flags = jnp.where(lane == which, flags[which, 6].astype(F32), root_flags)
    g2[...] = coef2
    for i in range(PLANE):
        sa[i, :, 0:RANK] = g2[ROWS * i : ROWS * (i + 1), :]
        sa[i, :, RANK:] = root_flags

    pl.semaphore_wait(barrier, PLANE - 1 + PLANES - 1 + 2)

    @pl.loop(1, PLANE)
    def _(step):
        other = (j + step) % PLANE
        copy(sa.at[other], e2.at[HALO + j], SEM_A, z * PLANE + other).start()

    e2[HALO + j] = sa[j]

    ppad[...] = jnp.zeros_like(ppad)
    ppad[0:3, :] = pts[...]
    side_copies = [
        copy(ppad, pside.at[0], SEM_PTS, right),
        copy(ppad, pside.at[1], SEM_PTS + 1, left),
        copy(vec, vside.at[0], SEM_VEC, right),
        copy(vec, vside.at[1], SEM_VEC + 1, left),
        copy(ex0.at[pl.ds(4, 2)], ex0.at[pl.ds(0, 2)], SEM_RIM0, right),
        copy(ex0.at[pl.ds(2, 2)], ex0.at[pl.ds(6, 2)], SEM_RIM0 + 1, left),
        copy(ex1.at[pl.ds(2, 2)], ex1.at[pl.ds(0, 2)], SEM_RIM1, right),
        copy(ex1.at[pl.ds(2, 2)], ex1.at[pl.ds(4, 2)], SEM_RIM1 + 1, left),
    ]
    for item in side_copies:
        item.start()

    prox_rows = prox[...]
    prox_cols = jnp.concatenate([prox_rows, jnp.zeros((5, RANK), F32)], axis=0).T
    gf[...] = prox_cols

    for axis in range(3):
        side = 2.0 ** ((axis - TOP) / 3.0)
        for place, offset in enumerate((2.0, 3.0)):
            for step in range(RANK // CHUNK):
                rows = slice(step * CHUNK, (step + 1) * CHUNK)
                squared = None
                for c in range(3):
                    column = gf[rows, c : c + 1]
                    if c == axis:
                        column = column - offset
                    delta = column - prox_rows[c : c + 1, :]
                    squared = delta * delta if squared is None else squared + delta * delta
                distance = squared * lax.rsqrt(jnp.maximum(squared, 1e-30))
                u = distance * (ROOT_THREE / SHORT_SCALE * side)
                v = distance * (ROOT_THREE / LONG_SCALE * side)
                eu = jnp.exp2(u * -LOG2_E)
                ev = jnp.exp2(v * -LOG2_E)
                for third in range(3):
                    value = (1.0 + u) * eu + (1.0 + v) * ev
                    head, rest = head_and_rest(value)
                    at = 2 * (axis + 3 * third) + place
                    ch[at, rows, :] = head
                    cl[at, rows, :] = rest
                    if third < 2:
                        u, v, eu, ev = u + u, v + v, eu * eu, ev * ev

    def field(level, minus, plus, even, odd, rows):
        two, three = 2 * level, 2 * level + 1
        first = mul(halves(minus), ch[two], cl[two])
        second = mul(halves(plus), ch[two], cl[two], TRANSPOSED)
        even_part = mul(halves(even), ch[three], cl[three], TRANSPOSED)
        odd_part = mul(halves(odd), ch[three], cl[three])
        if rows is None:
            return first, second, even_part, odd_part
        return (first + second + stack(even_part, odd_part, rows)) * (1.0 / 32.0)

    gm[...] = jnp.zeros_like(gm)
    gp[...] = jnp.zeros_like(gp)
    ge[...] = jnp.zeros_like(ge)
    go[...] = jnp.zeros_like(go)

    def columns_of(window, points):
        cols[window] = points.T

    def evaluate(reader, window, slot):
        reader_rows = ppad[:, pl.ds(pl.multiple_of(reader * LEAF, LEAF), LEAF)]
        for step in range(LEAF // CHUNK):
            rows = slice(step * CHUNK, (step + 1) * CHUNK)
            squared = None
            for c in range(3):
                delta = cols[window, rows, c : c + 1] - reader_rows[c : c + 1, :]
                squared = delta * delta if squared is None else squared + delta * delta
            distance = squared * lax.rsqrt(jnp.maximum(squared, 1e-30))
            short, long = ROOT_THREE / SHORT_SCALE, ROOT_THREE / LONG_SCALE
            value = (1.0 + distance * short) * jnp.exp2(distance * (-LOG2_E * short))
            value = value + (1.0 + distance * long) * jnp.exp2(distance * (-LOG2_E * long))
            head, rest = head_and_rest(value)
            kh[slot, rows, :] = head
            kl[slot, rows, :] = rest

    def amount(reader, window):
        target = me * LEAVES + window - 4
        total = jnp.float32(0.0)
        for slot in range(8):
            hit = jnp.logical_and(slot < cnt[reader], src[reader, slot] == target)
            total = total + jnp.where(hit, 1.0, 0.0)
        return total

    def gather_near(reader, window, slot, dims):
        near[reader] += amount(reader, window) * mul(vhl[window], kh[slot], kl[slot], dims)

    near[...] = jnp.zeros_like(near)
    for leaf in range(LEAVES):
        columns_of(4 + leaf, ppad[:, leaf * LEAF : (leaf + 1) * LEAF])

    def local_pairs(pairs):
        for place in range(len(pairs) + 1):
            if place < len(pairs):
                first, second = pairs[place]
                evaluate(first, 4 + second, place % 2)
            if place > 0:
                first, second = pairs[place - 1]
                gather_near(first, 4 + second, (place - 1) % 2, NORMAL)
                if first != second:
                    gather_near(second, 4 + first, (place - 1) % 2, TRANSPOSED)

    every = [(a, b) for a in range(LEAVES) for b in range(a, LEAVES)]
    local_pairs(every[:5])

    copy(sa.at[pl.ds(0, PLANE - 1)], e2.at[pl.ds(HALO, PLANE - 1)], SEM_A, left).wait_recv()
    edge_copies = []

    def send_edges(level):
        ref, nodes = edge_of[level], nodes_at(level)
        width = min(HALO, nodes)
        at = SEM_EDGE + 2 * (level - 2)
        for item in (
            copy(
                ref.at[pl.ds(HALO + nodes - width, width)],
                ref.at[pl.ds(HALO - width, width)],
                at,
                above,
            ),
            copy(ref.at[pl.ds(HALO, width)], ref.at[pl.ds(HALO + nodes, width)], at + 1, below),
        ):
            item.start()
            edge_copies.append(item)

    send_edges(2)
    for p in range(PLANE):
        g2[ROWS * p : ROWS * (p + 1), :] = e2[HALO + reversed_bits(p, 5), :, 0:RANK]
    current = g2[...]
    for level in (3, 4, 5, 6, 7):
        rows = ROWS * nodes_at(level)
        both = jnp.concatenate([current[: max(rows, 8)], second_half(current, rows)], axis=1)
        current = parents(both)
        if level < 7:
            count = 7 - level
            for p in range(nodes_at(level)):
                edge_of[level][HALO + reversed_bits(p, count)] = current[ROWS * p : ROWS * (p + 1)]
            send_edges(level)
    s7[...] = current[0:ROWS]

    @pl.loop(1, PLANES)
    def _(step):
        other = (z + step) % PLANES
        copy(s7, top7.at[HALO + z], SEM_TOP, other * PLANE + j).start()

    top7[HALO + z] = s7[...]
    top7[0:HALO] = jnp.zeros((HALO, ROWS, RANK), F32)
    top7[HALO + PLANES :] = jnp.zeros((HALO, ROWS, RANK), F32)
    top8[...] = jnp.zeros_like(top8)

    local_pairs(every[5:])

    inside_below = jnp.where(z > 0, 1.0, 0.0)
    inside_above = jnp.where(z < PLANES - 1, 1.0, 0.0)
    for item in edge_copies:
        item.wait_recv()

    def plane_field(level):
        ref, nodes = edge_of[level], nodes_at(level)
        count = 7 - level

        def at(node):
            value = ref[HALO + node, :, 0:RANK]
            if node < 0:
                value = value * inside_below
            if node >= nodes:
                value = value * inside_above
            return value

        for p in range(nodes):
            node = reversed_bits(p, count)
            rows = slice(ROWS * p, ROWS * (p + 1))
            gm[rows, :] = at(node - 2)
            gp[rows, :] = at(node + 2)
            if p < nodes // 2:
                ge[rows, :] = at(node + 3)
            else:
                half = p - nodes // 2
                go[ROWS * half : ROWS * (half + 1), :] = at(node - 3)
            if level == 2:
                gf[rows, :] = ref[HALO + node, :, RANK : RANK + 8]
        size = max(ROWS * nodes, 8)
        half_size = max(ROWS * nodes // 2, 8)
        minus, plus = gm[0:size, :], gp[0:size, :]
        even, odd = ge[0:half_size, :], go[0:half_size, :]
        if level == 2:
            weights = gf[0:size, :]
            minus = minus * weights[:, 0:1]
            plus = plus * weights[:, 1:2]
            even = even * weights[:half_size, 2:3]
            odd = odd * weights[half_size:, 2:3]
        fs[level - 2, 0:size, :] = field(level, minus, plus, even, odd, ROWS * nodes // 2)

    for level in PLANE_LEVELS:
        plane_field(level)

    copy(
        top7.at[pl.ds(HALO, PLANES - 1)], top7.at[pl.ds(HALO, PLANES - 1)], SEM_TOP, left
    ).wait_recv()
    for p in range(PLANES):
        g2[ROWS * p : ROWS * (p + 1), :] = top7[HALO + reversed_bits(p, 3)]
    coef8 = parents(jnp.concatenate([g2[0:8, :], g2[8:16, :]], axis=1))
    for p in range(4):
        top8[HALO + reversed_bits(p, 2)] = coef8[ROWS * p : ROWS * (p + 1)]

    def own_field(level, ref, node):
        parity = node % 2
        gm[0:ROWS, :] = ref[HALO + node - 2]
        gp[0:ROWS, :] = ref[HALO + node + 2]
        ge[0:ROWS, :] = ref[jnp.where(parity == 0, HALO + node + 3, HALO + node - 3)]
        third = ge[0:8, :]
        first, second, even, odd = field(level, gm[0:8, :], gp[0:8, :], third, third, None)
        return (first + second + jnp.where(parity == 0, even, odd)) * (1.0 / 32.0)

    def children(parent):
        return mul(halves(parent), th[...], tl[...], TRANSPOSED)

    field7 = own_field(7, top7, z)
    down = own_field(8, top8, z // 2)
    both = children(down)
    down = field7 + jnp.where(z % 2 == 0, both[:, :RANK], both[:, RANK:])
    for level in (6, 5, 4, 3, 2):
        size = max(ROWS * nodes_at(level), 8)
        both = children(down)
        rows = ROWS * nodes_at(level) // 2
        down = fs[level - 2, 0:size, :] + stack(both[:, :RANK], both[:, RANK:], rows)
    for p in range(PLANE):
        sb[reversed_bits(p, 5)] = down[ROWS * p : ROWS * (p + 1)]

    @pl.loop(1, PLANE)
    def _(step):
        other = (j + step) % PLANE
        copy(sb.at[other], rb.at[j], SEM_B, z * PLANE + other).start()

    rb[j] = sb[j]

    for item in side_copies:
        item.wait_recv()
    has_left = jnp.where(me > 0, 1.0, 0.0)
    has_right = jnp.where(me < DEVICES - 1, 1.0, 0.0)

    def local_field(level, ref, nodes, first_row, target):
        def at(node, which, reader):
            weight = flags[which, first_row + reader].astype(F32)
            if node < 0:
                weight = weight * has_left
            if node >= nodes:
                weight = weight * has_right
            return ref[2 + node] * weight

        order = list(range(0, nodes, 2)) + list(range(1, nodes, 2))
        minus = jnp.concatenate([at(n - 2, 0, n) for n in order], axis=0)
        plus = jnp.concatenate([at(n + 2, 1, n) for n in order], axis=0)
        even = jnp.concatenate([at(n + 3, 2, n) for n in range(0, nodes, 2)], axis=0)
        odd = jnp.concatenate([at(n - 3, 2, n) for n in range(1, nodes, 2)], axis=0)
        value = field(level, minus, plus, even, odd, RHS * nodes // 2)
        for place, n in enumerate(order):
            target[n] = value[RHS * place : RHS * (place + 1)]

    local_field(0, ex0, LEAVES, 0, f0)
    local_field(1, ex1, LEAVES // 2, LEAVES, f1)

    for leaf in range(LEAVES):
        lanes = slice(leaf * LEAF, (leaf + 1) * LEAF)
        vhl[leaf] = halves(vside[0, :, lanes])
        vhl[8 + leaf] = halves(vside[1, :, lanes])
        columns_of(leaf, pside[0, :, lanes])
        columns_of(8 + leaf, pside[1, :, lanes])

    def place_of(index):
        reader = index // 5
        step = index % 5
        return reader, reader + step + jnp.where(step < 4 - reader, 0, 4)

    pairs_count = 5 * LEAVES
    evaluate(0, 0, 1)

    @pl.loop(0, pairs_count // 2 - 1)
    def _(step):
        evaluate(*place_of(2 * step + 1), 0)
        gather_near(*place_of(2 * step), 1, NORMAL)
        evaluate(*place_of(2 * step + 2), 1)
        gather_near(*place_of(2 * step + 1), 0, NORMAL)

    evaluate(*place_of(pairs_count - 1), 0)
    gather_near(*place_of(pairs_count - 2), 1, NORMAL)
    gather_near(*place_of(pairs_count - 1), 0, NORMAL)

    copy(sb.at[pl.ds(0, PLANE - 1)], rb.at[pl.ds(0, PLANE - 1)], SEM_B, left).wait_recv()
    for i in range(PLANE):
        g2[ROWS * i : ROWS * (i + 1), :] = rb[i]
    both = children(g2[...])
    down1 = jnp.concatenate([f1[0] + both[:, :RANK], f1[1] + both[:, RANK:]], axis=0)
    both = children(down1)
    for leaf in range(LEAVES):
        lanes = slice(leaf * LEAF, (leaf + 1) * LEAF)
        part = both[RHS * (leaf // 2) : RHS * (leaf // 2 + 1)]
        part = part[:, RANK * (leaf % 2) : RANK * (leaf % 2 + 1)]
        far = mul(halves(f0[leaf] + part), bh[:, lanes], bl[:, lanes])
        own = noise[:, lanes] * vec[:, lanes]
        out[:, lanes] = own + far + near[leaf] * (1.0 / 32.0)

    copy(sa.at[pl.ds(0, PLANE - 1)], e2.at[pl.ds(HALO, PLANE - 1)], SEM_A, left).wait_send()
    copy(sb.at[pl.ds(0, PLANE - 1)], rb.at[pl.ds(0, PLANE - 1)], SEM_B, left).wait_send()
    copy(
        top7.at[pl.ds(HALO, PLANES - 1)], top7.at[pl.ds(HALO, PLANES - 1)], SEM_TOP, left
    ).wait_send()
    for item in side_copies + edge_copies:
        item.wait_send()


def on_device(vectors, points, noise, bases, transfer, proxies, near_src, near_count, far_flags):
    vmem = pl.BlockSpec(memory_space=pltpu.VMEM)
    width = RANK + 128

    def buffer(*shape, dtype=F32):
        return pltpu.VMEM(shape, dtype)

    points_count = LEAVES * LEAF
    scratch = [
        buffer(RHS, points_count),
        buffer(3, points_count),
        buffer(1, points_count),
        buffer(RANK, points_count),
        buffer(2, RANK, RANK),
        buffer(3, RANK),
        pltpu.SMEM((LEAVES, 8), jnp.int32),
        pltpu.SMEM((LEAVES,), jnp.int32),
        pltpu.SMEM((3, 2 * LEAVES - 1), jnp.int32),
        buffer(12, 2 * RHS, LEAF, dtype=BF16),
        buffer(RANK, LEAVES * LEAF, dtype=BF16),
        buffer(RANK, LEAVES * LEAF, dtype=BF16),
        buffer(2 * RANK, RANK, dtype=BF16),
        buffer(2 * RANK, RANK, dtype=BF16),
        buffer(2, RHS, LEAVES * LEAF),
        buffer(8, LEAVES * LEAF),
        buffer(2, 8, LEAVES * LEAF),
        buffer(12, LEAF, 8),
        buffer(2, LEAF, LEAF, dtype=BF16),
        buffer(2, LEAF, LEAF, dtype=BF16),
        buffer(18, RANK, RANK, dtype=BF16),
        buffer(18, RANK, RANK, dtype=BF16),
        buffer(LEAVES, RHS, LEAF),
        buffer(LEAVES + 4, RHS, RANK),
        buffer(LEAVES // 2 + 4, RHS, RANK),
        buffer(LEAVES, RHS, RANK),
        buffer(LEAVES // 2, RHS, RANK),
        buffer(PLANE, ROWS, width),
        buffer(PLANE, ROWS, RANK),
        buffer(PLANE, ROWS, RANK),
        buffer(ROWS, RANK),
        buffer(PLANE + 2 * HALO, ROWS, width),
    ]
    for level in PLANE_LEVELS[1:]:
        scratch.append(buffer(nodes_at(level) + 2 * HALO, ROWS, RANK))
    scratch += [
        buffer(PLANES + 2 * HALO, ROWS, RANK),
        buffer(4 + 2 * HALO, ROWS, RANK),
        buffer(RHS, RANK),
        buffer(RHS, RANK),
        buffer(RHS, RANK),
        buffer(RHS, RANK),
        buffer(RANK, 8),
        buffer(RHS, RANK),
        buffer(len(PLANE_LEVELS), RHS, RANK),
        pltpu.SemaphoreType.DMA((9,)),
        pltpu.SemaphoreType.DMA((SEMS,)),
        pltpu.SemaphoreType.DMA((SEMS,)),
    ]
    return pl.pallas_call(
        kernel,
        out_shape=jax.ShapeDtypeStruct(vectors.shape, F32),
        in_specs=[pl.BlockSpec(memory_space=pltpu.HBM)] * 9,
        out_specs=vmem,
        scratch_shapes=scratch,
        compiler_params=pltpu.CompilerParams(
            collective_id=0, has_side_effects=True, vmem_limit_bytes=62 * 2**20
        ),
        cost_estimate=pl.CostEstimate(
            flops=3 * 10**9, bytes_accessed=3 * 10**6, transcendentals=10**7
        ),
    )(
        vectors,
        points,
        noise.reshape(1, -1),
        bases,
        transfer,
        proxies,
        near_src,
        near_count,
        far_flags.T,
    )


def solution(mesh):
    in_specs = (
        P(None, "leaf"),
        P(None, "leaf"),
        P("leaf"),
        P(None, "leaf"),
        P(),
        P(),
        P("leaf", None),
        P("leaf"),
        P("leaf", None),
    )
    return jax.shard_map(
        on_device, mesh=mesh, in_specs=in_specs, out_specs=P(None, "leaf"), check_vma=False
    )
```

```python
import functools
import math

import jax
import jax.numpy as jnp
from jax import lax
from jax.experimental import pallas as pl
from jax.experimental.pallas import tpu as pltpu
from jax.sharding import PartitionSpec as P

SHORT_SCALE = 0.02
LONG_SCALE = 1.0
ROOT_THREE = 1.7320508075688772
LOG2_E = 1.4426950408889634

F32 = jnp.float32
BF16 = jnp.bfloat16
MESH = pl.DeviceIdType.MESH

LEAVES = 4
LEAF = 256
RANK = 256
RHS = 64
ROWS = 2
PLANE = 32
PLANES = 8
DEVICES = PLANE * PLANES
TOP = 10
HALO = 3
CHUNK = 32
LOCAL_FIRST = 4
LOCAL_CHAIN = 4
CHAIN_PAIRS = ((0,), (1,), (2,), (3,), (4,))
FIELD_PAIRS = 4

NORMAL = (((1,), (0,)), ((), ()))
TRANSPOSED = (((1,), (1,)), ((), ()))

PLANE_LEVELS = (2, 3, 4, 5, 6)

PLANE_ORDER = sorted(
    range(1, PLANE), key=lambda s: -(min(s // 8, 4 - s // 8) + min(s // 2 % 4, 4 - s // 2 % 4))
)
COLUMN_ORDER = (4, 3, 5, 2, 6, 1, 7)

SEM_A, SEM_TOP, SEM_B = 0, 1, 2
SEM_VEC, SEM_PTS, SEM_RIM0, SEM_RIM1, SEM_EDGE = 3, 5, 7, 9, 11
SEMS = SEM_EDGE + 2 * len(PLANE_LEVELS)


def nodes_at(level):
    return PLANE >> (level - 2)


def reversed_bits(value, count):
    result = 0
    for bit in range(count):
        result = result * 2 + (value >> bit & 1)
    return result


def halves(x):
    head = x.astype(BF16).astype(F32)
    return jnp.concatenate([head, x - head], axis=0).astype(BF16)


def head_and_rest(x):
    head = x.astype(BF16)
    return head, (x - head.astype(F32)).astype(BF16)


def mul(stacked, w_head, w_rest, dims=NORMAL):
    rows = stacked.shape[0] // 2
    if rows % 16 == 0:
        first = lax.dot_general(stacked, w_head, dims, preferred_element_type=F32)
        second = lax.dot_general(stacked[:rows], w_rest, dims, preferred_element_type=F32)
        return first[:rows] + first[rows:] + second
    both = lax.dot_general(stacked, w_head, dims, preferred_element_type=F32)
    both = both + lax.dot_general(stacked, w_rest, dims, preferred_element_type=F32)
    return both[:rows] + both[rows:]


def stack(first, second, rows):
    if rows % 8 == 0:
        return jnp.concatenate([first[:rows], second[:rows]], axis=0)
    place = lax.broadcasted_iota(jnp.int32, first.shape, 0)
    return jnp.where(place < rows, first, pltpu.roll(second, rows, 0))


def second_half(x, rows):
    if rows % 8 == 0:
        return x[rows:]
    return pltpu.roll(x, x.shape[0] - rows, 0)


def kernel(
    vec_in,
    pts_in,
    noise_in,
    bases_in,
    transfer_in,
    prox_in,
    src_in,
    cnt_in,
    flags_in,
    out,
    vec,
    pts,
    noise,
    bases,
    transfer,
    prox,
    src,
    cnt,
    flags,
    vhl,
    bh,
    bl,
    th,
    tl,
    vside,
    ppad,
    pside,
    cols,
    kh,
    kl,
    ch,
    cl,
    near,
    ex0,
    ex1,
    f0,
    f1,
    sa,
    sb,
    rb,
    s7,
    e2,
    e3,
    e4,
    e5,
    e6,
    top7,
    top8,
    gm,
    gp,
    ge,
    go,
    gf,
    g2,
    fs,
    load,
    send,
    recv,
):
    loads = [
        pltpu.make_async_copy(source, target, load.at[place])
        for place, (source, target) in enumerate(
            (
                (vec_in, vec),
                (bases_in, bases),
                (transfer_in, transfer),
                (pts_in, pts),
                (prox_in, prox),
                (noise_in, noise),
                (src_in, src),
                (cnt_in, cnt),
                (flags_in, flags),
            )
        )
    ]
    edge_of = {2: e2, 3: e3, 4: e4, 5: e5, 6: e6}
    me = lax.axis_index("leaf")
    z, j = me // PLANE, me % PLANE
    left = (me + DEVICES - 1) % DEVICES
    right = (me + 1) % DEVICES
    below = (me + DEVICES - PLANE) % DEVICES
    above = (me + PLANE) % DEVICES

    barrier = pltpu.get_barrier_semaphore()

    def greet(device):
        pl.semaphore_signal(barrier, inc=1, device_id=(device,), device_id_type=MESH)

    def in_plane(step):
        return lax.rem(j + step, PLANE)

    def in_column(step):
        return lax.rem(z + step, PLANES)

    for step in PLANE_ORDER:
        greet(z * PLANE + in_plane(step))
    for step in COLUMN_ORDER:
        greet(in_column(step) * PLANE + j)
    greet(left)
    greet(right)
    for item in loads:
        item.start()

    def copy(source, target, sem, device):
        return pltpu.make_async_remote_copy(
            src_ref=source,
            dst_ref=target,
            send_sem=send.at[sem],
            recv_sem=recv.at[sem],
            device_id=(device,),
            device_id_type=MESH,
        )

    for item in loads:
        item.wait()
    head, rest = head_and_rest(transfer[...].reshape(2 * RANK, RANK))
    th[...] = head
    tl[...] = rest
    coef0 = []
    for leaf in range(LEAVES):
        lanes = slice(leaf * LEAF, (leaf + 1) * LEAF)
        head, rest = head_and_rest(bases[:, lanes])
        bh[:, lanes] = head
        bl[:, lanes] = rest
        pair = halves(vec[:, lanes])
        vhl[4 + leaf] = pair
        value = mul(pair, head, rest, TRANSPOSED)
        ex0[2 + leaf] = value
        coef0.append(value)

    def parents(children):
        return mul(halves(children), th[...], tl[...])

    pair_rows = [jnp.concatenate([coef0[2 * n], coef0[2 * n + 1]], axis=1) for n in range(2)]
    coef1 = parents(jnp.concatenate(pair_rows, axis=0))
    ex1[2] = coef1[:RHS]
    ex1[3] = coef1[RHS:]
    coef2 = parents(jnp.concatenate([coef1[:RHS], coef1[RHS:]], axis=1))

    lane = lax.broadcasted_iota(jnp.int32, (ROWS, 128), 1)
    root_flags = jnp.zeros((ROWS, 128), F32)
    for which in range(3):
        root_flags = jnp.where(lane == which, flags[which, 6].astype(F32), root_flags)
    g2[...] = coef2
    for i in range(PLANE):
        sa[i, :, 0:RANK] = g2[ROWS * i : ROWS * (i + 1), :]
        sa[i, :, RANK:] = root_flags

    pl.semaphore_wait(barrier, PLANE - 1 + PLANES - 1 + 2)

    for step in PLANE_ORDER:
        other = in_plane(step)
        copy(sa.at[other], e2.at[HALO + j], SEM_A, z * PLANE + other).start()

    e2[HALO + j] = sa[j]

    ppad[...] = jnp.zeros_like(ppad)
    ppad[0:3, :] = pts[...]
    side_copies = [
        copy(ppad, pside.at[0], SEM_PTS, right),
        copy(ppad, pside.at[1], SEM_PTS + 1, left),
        copy(vec, vside.at[0], SEM_VEC, right),
        copy(vec, vside.at[1], SEM_VEC + 1, left),
        copy(ex0.at[pl.ds(4, 2)], ex0.at[pl.ds(0, 2)], SEM_RIM0, right),
        copy(ex0.at[pl.ds(2, 2)], ex0.at[pl.ds(6, 2)], SEM_RIM0 + 1, left),
        copy(ex1.at[pl.ds(2, 2)], ex1.at[pl.ds(0, 2)], SEM_RIM1, right),
        copy(ex1.at[pl.ds(2, 2)], ex1.at[pl.ds(4, 2)], SEM_RIM1 + 1, left),
    ]
    prox_rows = prox[...]
    prox_cols = jnp.concatenate([prox_rows, jnp.zeros((5, RANK), F32)], axis=0).T
    gf[...] = prox_cols

    for axis in range(3):
        side = 2.0 ** ((axis - TOP) / 3.0)
        for place, offset in enumerate((2.0, 3.0)):
            for step in range(RANK // CHUNK):
                rows = slice(step * CHUNK, (step + 1) * CHUNK)
                squared = None
                for c in range(3):
                    column = gf[rows, c : c + 1]
                    if c == axis:
                        column = column - offset
                    delta = column - prox_rows[c : c + 1, :]
                    squared = delta * delta if squared is None else squared + delta * delta
                distance = squared * lax.rsqrt(jnp.maximum(squared, 1e-30))
                u = distance * (ROOT_THREE / SHORT_SCALE * side)
                v = distance * (ROOT_THREE / LONG_SCALE * side)
                eu = jnp.exp2(u * -LOG2_E)
                ev = jnp.exp2(v * -LOG2_E)
                for third in range(3):
                    value = (1.0 + u) * eu + (1.0 + v) * ev
                    head, rest = head_and_rest(value)
                    at = 2 * (axis + 3 * third) + place
                    ch[at, rows, :] = head
                    cl[at, rows, :] = rest
                    if third < 2:
                        u, v, eu, ev = u + u, v + v, eu * eu, ev * ev

    def field(level, minus, plus, even, odd, rows):
        two, three = 2 * level, 2 * level + 1
        first = mul(halves(minus), ch[two], cl[two])
        second = mul(halves(plus), ch[two], cl[two], TRANSPOSED)
        even_part = mul(halves(even), ch[three], cl[three], TRANSPOSED)
        odd_part = mul(halves(odd), ch[three], cl[three])
        if rows is None:
            return first, second, even_part, odd_part
        return (first + second + stack(even_part, odd_part, rows)) * (1.0 / 32.0)

    top7[0:HALO] = jnp.zeros((HALO, ROWS, RANK), F32)
    top7[HALO + PLANES :] = jnp.zeros((HALO, ROWS, RANK), F32)
    top8[...] = jnp.zeros_like(top8)
    gm[...] = jnp.zeros_like(gm)
    gp[...] = jnp.zeros_like(gp)
    ge[...] = jnp.zeros_like(ge)
    go[...] = jnp.zeros_like(go)

    def columns_of(window, points):
        cols[window] = points.T

    def evaluate(reader, window, slot):
        reader_rows = ppad[:, pl.ds(pl.multiple_of(reader * LEAF, LEAF), LEAF)]
        for step in range(LEAF // CHUNK):
            rows = slice(step * CHUNK, (step + 1) * CHUNK)
            squared = None
            for c in range(3):
                delta = cols[window, rows, c : c + 1] - reader_rows[c : c + 1, :]
                squared = delta * delta if squared is None else squared + delta * delta
            distance = squared * lax.rsqrt(jnp.maximum(squared, 1e-30))
            short, long = ROOT_THREE / SHORT_SCALE, ROOT_THREE / LONG_SCALE
            value = (1.0 + distance * short) * jnp.exp2(distance * (-LOG2_E * short))
            value = value + (1.0 + distance * long) * jnp.exp2(distance * (-LOG2_E * long))
            head, rest = head_and_rest(value)
            kh[slot, rows, :] = head
            kl[slot, rows, :] = rest

    def amount(reader, window):
        target = me * LEAVES + window - 4
        total = jnp.float32(0.0)
        for slot in range(8):
            hit = jnp.logical_and(slot < cnt[reader], src[reader, slot] == target)
            total = total + jnp.where(hit, 1.0, 0.0)
        return total

    def gather_near(reader, window, slot, dims):
        near[reader] += amount(reader, window) * mul(vhl[window], kh[slot], kl[slot], dims)

    near[...] = jnp.zeros_like(near)
    for leaf in range(LEAVES):
        columns_of(4 + leaf, ppad[:, leaf * LEAF : (leaf + 1) * LEAF])

    def spread(pair, slot):
        first, second = pair
        gather_near(first, 4 + second, slot, NORMAL)
        if first != second:
            gather_near(second, 4 + first, slot, TRANSPOSED)

    def local_pairs(pairs):
        for place in range(len(pairs) + 1):
            if place < len(pairs):
                first, second = pairs[place]
                evaluate(first, 4 + second, place % 2)
            if place > 0:
                spread(pairs[place - 1], (place - 1) % 2)

    every = [(a, b) for a in range(LEAVES) for b in range(a, LEAVES)]
    local_pairs(every[:LOCAL_FIRST])

    copy(sa.at[pl.ds(0, PLANE - 1)], e2.at[pl.ds(HALO, PLANE - 1)], SEM_A, left).wait_recv()
    for item in side_copies[:4]:
        item.start()
    edge_copies = []

    def send_edges(level):
        ref, nodes = edge_of[level], nodes_at(level)
        width = min(HALO, nodes)
        at = SEM_EDGE + 2 * (level - 2)
        for item in (
            copy(
                ref.at[pl.ds(HALO + nodes - width, width)],
                ref.at[pl.ds(HALO - width, width)],
                at,
                above,
            ),
            copy(ref.at[pl.ds(HALO, width)], ref.at[pl.ds(HALO + nodes, width)], at + 1, below),
        ):
            item.start()
            edge_copies.append(item)

    for p in range(PLANE):
        g2[ROWS * p : ROWS * (p + 1), :] = e2[HALO + reversed_bits(p, 5), :, 0:RANK]
    current = g2[...]
    for level in (3, 4, 5, 6, 7):
        rows = ROWS * nodes_at(level)
        both = jnp.concatenate([current[: max(rows, 8)], second_half(current, rows)], axis=1)
        current = parents(both)
        if level < 7:
            count = 7 - level
            for p in range(nodes_at(level)):
                edge_of[level][HALO + reversed_bits(p, count)] = current[ROWS * p : ROWS * (p + 1)]
            if level - 3 < LOCAL_CHAIN:
                pair = every[LOCAL_FIRST + level - 3]
                evaluate(pair[0], 4 + pair[1], level % 2)
                spread(pair, level % 2)
    s7[...] = current[0:ROWS]

    for step in COLUMN_ORDER:
        copy(s7, top7.at[HALO + z], SEM_TOP, in_column(step) * PLANE + j).start()
    for level in PLANE_LEVELS:
        send_edges(level)
    for item in side_copies[4:]:
        item.start()
    middle = every[LOCAL_FIRST + LOCAL_CHAIN :]
    local_pairs(middle)

    top7[HALO + z] = s7[...]

    inside_below = jnp.where(z > 0, 1.0, 0.0)
    inside_above = jnp.where(z < PLANES - 1, 1.0, 0.0)
    for item in edge_copies:
        item.wait_recv()

    def plane_field(level):
        ref, nodes = edge_of[level], nodes_at(level)
        count, slot = 7 - level, level - 2

        def at(node):
            value = ref[HALO + node, :, 0:RANK]
            if node < 0:
                value = value * inside_below
            if node >= nodes:
                value = value * inside_above
            return value

        for p in range(nodes):
            node = reversed_bits(p, count)
            rows = slice(ROWS * p, ROWS * (p + 1))
            gm[slot, rows, :] = at(node - 2)
            gp[slot, rows, :] = at(node + 2)
            if p < nodes // 2:
                ge[slot, rows, :] = at(node + 3)
            else:
                half = p - nodes // 2
                go[slot, ROWS * half : ROWS * (half + 1), :] = at(node - 3)
            if level == 2:
                gf[rows, :] = ref[HALO + node, :, RANK : RANK + 8]
        size = max(ROWS * nodes, 8)
        half_size = max(ROWS * nodes // 2, 8)
        minus, plus = gm[slot, 0:size, :], gp[slot, 0:size, :]
        even, odd = ge[slot, 0:half_size, :], go[slot, 0:half_size, :]
        if level == 2:
            weights = gf[0:size, :]
            minus = minus * weights[:, 0:1]
            plus = plus * weights[:, 1:2]
            even = even * weights[:half_size, 2:3]
            odd = odd * weights[half_size:, 2:3]
        fs[level - 2, 0:size, :] = field(level, minus, plus, even, odd, ROWS * nodes // 2)

    for level in PLANE_LEVELS:
        plane_field(level)

    def take_sides():
        for item in side_copies[:4]:
            item.wait_recv()
        for leaf in range(LEAVES):
            lanes = slice(leaf * LEAF, (leaf + 1) * LEAF)
            vhl[leaf] = halves(vside[0, :, lanes])
            vhl[8 + leaf] = halves(vside[1, :, lanes])
            columns_of(leaf, pside[0, :, lanes])
            columns_of(8 + leaf, pside[1, :, lanes])

    def place_of(index):
        reader = index // 5
        step = index % 5
        return reader, reader + step + jnp.where(step < 4 - reader, 0, 4)

    def side_pairs(start, stop):
        evaluate(*place_of(start), 1)

        @pl.loop(0, (stop - start - 1) // 2)
        def _(step):
            index = start + 2 * step
            evaluate(*place_of(index + 1), 0)
            gather_near(*place_of(index), 1, NORMAL)
            evaluate(*place_of(index + 2), 1)
            gather_near(*place_of(index + 1), 0, NORMAL)

        if (stop - start) % 2 == 0:
            evaluate(*place_of(stop - 1), 0)
            gather_near(*place_of(stop - 2), 1, NORMAL)
            gather_near(*place_of(stop - 1), 0, NORMAL)
        else:
            gather_near(*place_of(stop - 1), 1, NORMAL)


    copy(
        top7.at[pl.ds(HALO, PLANES - 1)], top7.at[pl.ds(HALO, PLANES - 1)], SEM_TOP, left
    ).wait_recv()
    for p in range(PLANES):
        g2[ROWS * p : ROWS * (p + 1), :] = top7[HALO + reversed_bits(p, 3)]
    coef8 = parents(jnp.concatenate([g2[0:8, :], g2[8:16, :]], axis=1))
    for p in range(4):
        top8[HALO + reversed_bits(p, 2)] = coef8[ROWS * p : ROWS * (p + 1)]

    def own_field(level, ref, node):
        parity = node % 2
        slot = level - 2
        gm[slot, 0:ROWS, :] = ref[HALO + node - 2]
        gp[slot, 0:ROWS, :] = ref[HALO + node + 2]
        ge[slot, 0:ROWS, :] = ref[jnp.where(parity == 0, HALO + node + 3, HALO + node - 3)]
        third = ge[slot, 0:8, :]
        minus, plus = gm[slot, 0:8, :], gp[slot, 0:8, :]
        first, second, even, odd = field(level, minus, plus, third, third, None)
        return (first + second + jnp.where(parity == 0, even, odd)) * (1.0 / 32.0)

    def children(parent):
        return mul(halves(parent), th[...], tl[...], TRANSPOSED)

    field7 = own_field(7, top7, z)
    down = own_field(8, top8, z // 2)
    both = children(down)
    down = field7 + jnp.where(z % 2 == 0, both[:, :RANK], both[:, RANK:])
    take_sides()
    for level in (6, 5, 4, 3, 2):
        size = max(ROWS * nodes_at(level), 8)
        both = children(down)
        rows = ROWS * nodes_at(level) // 2
        down = fs[level - 2, 0:size, :] + stack(both[:, :RANK], both[:, RANK:], rows)
        for pair in CHAIN_PAIRS[6 - level]:
            evaluate(*place_of(pair), pair % 2)
            gather_near(*place_of(pair), pair % 2, NORMAL)
    for p in range(PLANE):
        sb[reversed_bits(p, 5)] = down[ROWS * p : ROWS * (p + 1)]

    for step in PLANE_ORDER:
        other = in_plane(step)
        copy(sb.at[other], rb.at[j], SEM_B, z * PLANE + other).start()

    rb[j] = sb[j]

    done = sum(len(group) for group in CHAIN_PAIRS)
    side_pairs(done, 5 * LEAVES - FIELD_PAIRS)
    done = 5 * LEAVES - FIELD_PAIRS
    for item in side_copies[4:]:
        item.wait_recv()
    has_left = jnp.where(me > 0, 1.0, 0.0)
    has_right = jnp.where(me < DEVICES - 1, 1.0, 0.0)

    def local_field(level, ref, nodes, first_row, target):
        def at(node, which, reader):
            weight = flags[which, first_row + reader].astype(F32)
            if node < 0:
                weight = weight * has_left
            if node >= nodes:
                weight = weight * has_right
            return ref[2 + node] * weight

        order = list(range(0, nodes, 2)) + list(range(1, nodes, 2))
        minus = jnp.concatenate([at(n - 2, 0, n) for n in order], axis=0)
        plus = jnp.concatenate([at(n + 2, 1, n) for n in order], axis=0)
        even = jnp.concatenate([at(n + 3, 2, n) for n in range(0, nodes, 2)], axis=0)
        odd = jnp.concatenate([at(n - 3, 2, n) for n in range(1, nodes, 2)], axis=0)
        value = field(level, minus, plus, even, odd, RHS * nodes // 2)
        for place, n in enumerate(order):
            target[n] = value[RHS * place : RHS * (place + 1)]

    if FIELD_PAIRS:
        for item in range(FIELD_PAIRS + 1):
            if item < FIELD_PAIRS:
                evaluate(*place_of(done + item), item % 2)
            if item == 0:
                local_field(0, ex0, LEAVES, 0, f0)
            if item == 1:
                local_field(1, ex1, LEAVES // 2, LEAVES, f1)
            if item > 0:
                gather_near(*place_of(done + item - 1), (item - 1) % 2, NORMAL)
    else:
        local_field(0, ex0, LEAVES, 0, f0)
        local_field(1, ex1, LEAVES // 2, LEAVES, f1)

    copy(sb.at[pl.ds(0, PLANE - 1)], rb.at[pl.ds(0, PLANE - 1)], SEM_B, left).wait_recv()
    for i in range(PLANE):
        g2[ROWS * i : ROWS * (i + 1), :] = rb[i]
    both = children(g2[...])
    down1 = jnp.concatenate([f1[0] + both[:, :RANK], f1[1] + both[:, RANK:]], axis=0)
    both = children(down1)
    for leaf in range(LEAVES):
        lanes = slice(leaf * LEAF, (leaf + 1) * LEAF)
        part = both[RHS * (leaf // 2) : RHS * (leaf // 2 + 1)]
        part = part[:, RANK * (leaf % 2) : RANK * (leaf % 2 + 1)]
        far = mul(halves(f0[leaf] + part), bh[:, lanes], bl[:, lanes])
        own = noise[:, lanes] * vec[:, lanes]
        out[:, lanes] = own + far + near[leaf] * (1.0 / 32.0)

    copy(sa.at[pl.ds(0, PLANE - 1)], e2.at[pl.ds(HALO, PLANE - 1)], SEM_A, left).wait_send()
    copy(sb.at[pl.ds(0, PLANE - 1)], rb.at[pl.ds(0, PLANE - 1)], SEM_B, left).wait_send()
    copy(
        top7.at[pl.ds(HALO, PLANES - 1)], top7.at[pl.ds(HALO, PLANES - 1)], SEM_TOP, left
    ).wait_send()
    for item in side_copies + edge_copies:
        item.wait_send()


def on_device(vectors, points, noise, bases, transfer, proxies, near_src, near_count, far_flags):
    vmem = pl.BlockSpec(memory_space=pltpu.VMEM)
    width = RANK + 128

    def buffer(*shape, dtype=F32):
        return pltpu.VMEM(shape, dtype)

    points_count = LEAVES * LEAF
    scratch = [
        buffer(RHS, points_count),
        buffer(3, points_count),
        buffer(1, points_count),
        buffer(RANK, points_count),
        buffer(2, RANK, RANK),
        buffer(3, RANK),
        pltpu.SMEM((LEAVES, 8), jnp.int32),
        pltpu.SMEM((LEAVES,), jnp.int32),
        pltpu.SMEM((3, 2 * LEAVES - 1), jnp.int32),
        buffer(12, 2 * RHS, LEAF, dtype=BF16),
        buffer(RANK, LEAVES * LEAF, dtype=BF16),
        buffer(RANK, LEAVES * LEAF, dtype=BF16),
        buffer(2 * RANK, RANK, dtype=BF16),
        buffer(2 * RANK, RANK, dtype=BF16),
        buffer(2, RHS, LEAVES * LEAF),
        buffer(8, LEAVES * LEAF),
        buffer(2, 8, LEAVES * LEAF),
        buffer(12, LEAF, 8),
        buffer(2, LEAF, LEAF, dtype=BF16),
        buffer(2, LEAF, LEAF, dtype=BF16),
        buffer(18, RANK, RANK, dtype=BF16),
        buffer(18, RANK, RANK, dtype=BF16),
        buffer(LEAVES, RHS, LEAF),
        buffer(LEAVES + 4, RHS, RANK),
        buffer(LEAVES // 2 + 4, RHS, RANK),
        buffer(LEAVES, RHS, RANK),
        buffer(LEAVES // 2, RHS, RANK),
        buffer(PLANE, ROWS, width),
        buffer(PLANE, ROWS, RANK),
        buffer(PLANE, ROWS, RANK),
        buffer(ROWS, RANK),
        buffer(PLANE + 2 * HALO, ROWS, width),
    ]
    for level in PLANE_LEVELS[1:]:
        scratch.append(buffer(nodes_at(level) + 2 * HALO, ROWS, RANK))
    scratch += [
        buffer(PLANES + 2 * HALO, ROWS, RANK),
        buffer(4 + 2 * HALO, ROWS, RANK),
        buffer(7, RHS, RANK),
        buffer(7, RHS, RANK),
        buffer(7, RHS, RANK),
        buffer(7, RHS, RANK),
        buffer(RANK, 8),
        buffer(RHS, RANK),
        buffer(len(PLANE_LEVELS), RHS, RANK),
        pltpu.SemaphoreType.DMA((9,)),
        pltpu.SemaphoreType.DMA((SEMS,)),
        pltpu.SemaphoreType.DMA((SEMS,)),
    ]
    return pl.pallas_call(
        kernel,
        out_shape=jax.ShapeDtypeStruct(vectors.shape, F32),
        in_specs=[pl.BlockSpec(memory_space=pltpu.HBM)] * 9,
        out_specs=vmem,
        scratch_shapes=scratch,
        compiler_params=pltpu.CompilerParams(
            collective_id=0, has_side_effects=True, vmem_limit_bytes=62 * 2**20
        ),
        cost_estimate=pl.CostEstimate(
            flops=3 * 10**9, bytes_accessed=3 * 10**6, transcendentals=10**7
        ),
    )(
        vectors,
        points,
        noise.reshape(1, -1),
        bases,
        transfer,
        proxies,
        near_src,
        near_count,
        far_flags.T,
    )


def solution(mesh):
    in_specs = (
        P(None, "leaf"),
        P(None, "leaf"),
        P("leaf"),
        P(None, "leaf"),
        P(),
        P(),
        P("leaf", None),
        P("leaf"),
        P("leaf", None),
    )
    return jax.shard_map(
        on_device, mesh=mesh, in_specs=in_specs, out_specs=P(None, "leaf"), check_vma=False
    )
```

```python
import jax
import jax.numpy as jnp
from jax import lax
from jax.experimental import pallas as pl
from jax.experimental.pallas import tpu as pltpu
from jax.sharding import PartitionSpec as P

SHORT_SCALE = 0.02
LONG_SCALE = 1.0
ROOT_THREE = 1.7320508075688772
LOG2_E = 1.4426950408889634

F32 = jnp.float32
BF16 = jnp.bfloat16
MESH = pl.DeviceIdType.MESH

LEAVES = 4
LEAF = 256
RANK = 256
RHS = 64
ROWS = 2
PLANE = 32
PLANES = 8
DEVICES = PLANE * PLANES
TOP = 10
HALO = 3
CHUNK = 32
LOCAL_FIRST = 4
LOCAL_CHAIN = 4
CHAIN_PAIRS = ((0,), (1,), (2,), (3,), (4,))

NORMAL = (((1,), (0,)), ((), ()))
TRANSPOSED = (((1,), (1,)), ((), ()))

PLANE_LEVELS = (2, 3, 4, 5, 6)

PLANE_ORDER = sorted(
    range(1, PLANE), key=lambda s: -(min(s // 8, 4 - s // 8) + min(s // 2 % 4, 4 - s // 2 % 4))
)
COLUMN_ORDER = (4, 3, 5, 2, 6, 1, 7)

SEM_A, SEM_TOP, SEM_B = 0, 1, 2
SEM_VEC, SEM_PTS, SEM_RIM0, SEM_RIM1, SEM_FAR, SEM_EDGE = 3, 5, 7, 9, 11, 13
SEMS = SEM_EDGE + 2 * len(PLANE_LEVELS)


def nodes_at(level):
    return PLANE >> (level - 2)


def reversed_bits(value, count):
    result = 0
    for bit in range(count):
        result = result * 2 + (value >> bit & 1)
    return result


def halves(x):
    head = x.astype(BF16).astype(F32)
    return jnp.concatenate([head, x - head], axis=0).astype(BF16)


def head_and_rest(x):
    head = x.astype(BF16)
    return head, (x - head.astype(F32)).astype(BF16)


def mul(stacked, w_head, w_rest, dims=NORMAL):
    rows = stacked.shape[0] // 2
    if rows % 16 == 0:
        first = lax.dot_general(stacked, w_head, dims, preferred_element_type=F32)
        second = lax.dot_general(stacked[:rows], w_rest, dims, preferred_element_type=F32)
        return first[:rows] + first[rows:] + second
    both = lax.dot_general(stacked, w_head, dims, preferred_element_type=F32)
    both = both + lax.dot_general(stacked, w_rest, dims, preferred_element_type=F32)
    return both[:rows] + both[rows:]


def stack(first, second, rows):
    if rows % 8 == 0:
        return jnp.concatenate([first[:rows], second[:rows]], axis=0)
    place = lax.broadcasted_iota(jnp.int32, first.shape, 0)
    return jnp.where(place < rows, first, pltpu.roll(second, rows, 0))


def second_half(x, rows):
    if rows % 8 == 0:
        return x[rows:]
    return pltpu.roll(x, x.shape[0] - rows, 0)


def kernel(
    vec_in,
    pts_in,
    noise_in,
    bases_in,
    transfer_in,
    prox_in,
    src_in,
    cnt_in,
    flags_in,
    out,
    vec,
    pts,
    noise,
    bases,
    transfer,
    prox,
    src,
    cnt,
    flags,
    vhl,
    bh,
    bl,
    th,
    tl,
    vside,
    ppad,
    pside,
    cols,
    kh,
    kl,
    ch,
    cl,
    near,
    ex0,
    ex1,
    f0,
    f1,
    sa,
    sb,
    rb,
    s7,
    e2,
    e3,
    e4,
    e5,
    e6,
    top7,
    top8,
    gm,
    gp,
    ge,
    go,
    gf,
    g2,
    fs,
    load,
    send,
    recv,
):
    loads = [
        pltpu.make_async_copy(source, target, load.at[place])
        for place, (source, target) in enumerate(
            (
                (vec_in, vec),
                (bases_in, bases),
                (transfer_in, transfer),
                (pts_in, pts),
                (prox_in, prox),
                (noise_in, noise),
                (src_in, src),
                (cnt_in, cnt),
                (flags_in, flags),
            )
        )
    ]
    edge_of = {2: e2, 3: e3, 4: e4, 5: e5, 6: e6}
    me = lax.axis_index("leaf")
    z, j = me // PLANE, me % PLANE
    left = (me + DEVICES - 1) % DEVICES
    right = (me + 1) % DEVICES
    below = (me + DEVICES - PLANE) % DEVICES
    above = (me + PLANE) % DEVICES

    barrier = pltpu.get_barrier_semaphore()

    def greet(device):
        pl.semaphore_signal(barrier, inc=1, device_id=(device,), device_id_type=MESH)

    def in_plane(step):
        return lax.rem(j + step, PLANE)

    def in_column(step):
        return lax.rem(z + step, PLANES)

    for step in PLANE_ORDER:
        greet(z * PLANE + in_plane(step))
    for step in COLUMN_ORDER:
        greet(in_column(step) * PLANE + j)
    greet(left)
    greet(right)
    for item in loads:
        item.start()

    def copy(source, target, sem, device):
        return pltpu.make_async_remote_copy(
            src_ref=source,
            dst_ref=target,
            send_sem=send.at[sem],
            recv_sem=recv.at[sem],
            device_id=(device,),
            device_id_type=MESH,
        )

    for item in loads:
        item.wait()
    head, rest = head_and_rest(transfer[...].reshape(2 * RANK, RANK))
    th[...] = head
    tl[...] = rest
    coef0 = []
    for leaf in range(LEAVES):
        lanes = slice(leaf * LEAF, (leaf + 1) * LEAF)
        head, rest = head_and_rest(bases[:, lanes])
        bh[:, lanes] = head
        bl[:, lanes] = rest
        pair = halves(vec[:, lanes])
        vhl[4 + leaf] = pair
        value = mul(pair, head, rest, TRANSPOSED)
        ex0[2 + leaf] = value
        coef0.append(value)

    def parents(children):
        return mul(halves(children), th[...], tl[...])

    pair_rows = [jnp.concatenate([coef0[2 * n], coef0[2 * n + 1]], axis=1) for n in range(2)]
    coef1 = parents(jnp.concatenate(pair_rows, axis=0))
    ex1[2] = coef1[:RHS]
    ex1[3] = coef1[RHS:]
    coef2 = parents(jnp.concatenate([coef1[:RHS], coef1[RHS:]], axis=1))

    lane = lax.broadcasted_iota(jnp.int32, (ROWS, 128), 1)
    root_flags = jnp.zeros((ROWS, 128), F32)
    for which in range(3):
        root_flags = jnp.where(lane == which, flags[which, 6].astype(F32), root_flags)
    g2[...] = coef2
    for i in range(PLANE):
        sa[i, :, 0:RANK] = g2[ROWS * i : ROWS * (i + 1), :]
        sa[i, :, RANK:] = root_flags

    pl.semaphore_wait(barrier, PLANE - 1 + PLANES - 1 + 2)

    for step in PLANE_ORDER:
        other = in_plane(step)
        copy(sa.at[other], e2.at[HALO + j], SEM_A, z * PLANE + other).start()

    e2[HALO + j] = sa[j]

    ppad[...] = jnp.zeros_like(ppad)
    ppad[0:3, :] = pts[...]

    def side_copy(side, first, sem, device):
        lanes = pl.ds(first * LEAF, 2 * LEAF)
        return copy(vec.at[:, lanes], vside.at[side, :, lanes], sem, device)

    side_copies = [
        copy(ppad, pside.at[0], SEM_PTS, right),
        copy(ppad, pside.at[1], SEM_PTS + 1, left),
        side_copy(0, 2, SEM_VEC, right),
        side_copy(1, 0, SEM_VEC + 1, left),
        side_copy(0, 0, SEM_FAR, right),
        side_copy(1, 2, SEM_FAR + 1, left),
        copy(ex0.at[pl.ds(4, 2)], ex0.at[pl.ds(0, 2)], SEM_RIM0, right),
        copy(ex0.at[pl.ds(2, 2)], ex0.at[pl.ds(6, 2)], SEM_RIM0 + 1, left),
        copy(ex1.at[pl.ds(2, 2)], ex1.at[pl.ds(0, 2)], SEM_RIM1, right),
        copy(ex1.at[pl.ds(2, 2)], ex1.at[pl.ds(4, 2)], SEM_RIM1 + 1, left),
    ]
    prox_rows = prox[...]
    prox_cols = jnp.concatenate([prox_rows, jnp.zeros((5, RANK), F32)], axis=0).T
    gf[...] = prox_cols

    for axis in range(3):
        side = 2.0 ** ((axis - TOP) / 3.0)
        for place, offset in enumerate((2.0, 3.0)):
            for step in range(RANK // CHUNK):
                rows = slice(step * CHUNK, (step + 1) * CHUNK)
                squared = None
                for c in range(3):
                    column = gf[rows, c : c + 1]
                    if c == axis:
                        column = column - offset
                    delta = column - prox_rows[c : c + 1, :]
                    squared = delta * delta if squared is None else squared + delta * delta
                distance = squared * lax.rsqrt(jnp.maximum(squared, 1e-30))
                u = distance * (ROOT_THREE / SHORT_SCALE * side)
                v = distance * (ROOT_THREE / LONG_SCALE * side)
                eu = jnp.exp2(u * -LOG2_E)
                ev = jnp.exp2(v * -LOG2_E)
                for third in range(3):
                    value = (1.0 + u) * eu + (1.0 + v) * ev
                    head, rest = head_and_rest(value)
                    at = 2 * (axis + 3 * third) + place
                    ch[at, rows, :] = head
                    cl[at, rows, :] = rest
                    if third < 2:
                        u, v, eu, ev = u + u, v + v, eu * eu, ev * ev

    def field(level, minus, plus, even, odd, rows):
        two, three = 2 * level, 2 * level + 1
        first = mul(halves(minus), ch[two], cl[two])
        second = mul(halves(plus), ch[two], cl[two], TRANSPOSED)
        even_part = mul(halves(even), ch[three], cl[three], TRANSPOSED)
        odd_part = mul(halves(odd), ch[three], cl[three])
        if rows is None:
            return first, second, even_part, odd_part
        return (first + second + stack(even_part, odd_part, rows)) * (1.0 / 32.0)

    top7[0:HALO] = jnp.zeros((HALO, ROWS, RANK), F32)
    top7[HALO + PLANES :] = jnp.zeros((HALO, ROWS, RANK), F32)
    top8[...] = jnp.zeros_like(top8)
    gm[...] = jnp.zeros_like(gm)
    gp[...] = jnp.zeros_like(gp)
    ge[...] = jnp.zeros_like(ge)
    go[...] = jnp.zeros_like(go)

    def columns_of(window, points):
        cols[window] = points.T

    def evaluate(reader, window, slot):
        reader_rows = ppad[:, pl.ds(pl.multiple_of(reader * LEAF, LEAF), LEAF)]
        for step in range(LEAF // CHUNK):
            rows = slice(step * CHUNK, (step + 1) * CHUNK)
            squared = None
            for c in range(3):
                delta = cols[window, rows, c : c + 1] - reader_rows[c : c + 1, :]
                squared = delta * delta if squared is None else squared + delta * delta
            distance = squared * lax.rsqrt(jnp.maximum(squared, 1e-30))
            short, long = ROOT_THREE / SHORT_SCALE, ROOT_THREE / LONG_SCALE
            value = (1.0 + distance * short) * jnp.exp2(distance * (-LOG2_E * short))
            value = value + (1.0 + distance * long) * jnp.exp2(distance * (-LOG2_E * long))
            head, rest = head_and_rest(value)
            kh[slot, rows, :] = head
            kl[slot, rows, :] = rest

    def amount(reader, window):
        target = me * LEAVES + window - 4
        total = jnp.float32(0.0)
        for slot in range(8):
            hit = jnp.logical_and(slot < cnt[reader], src[reader, slot] == target)
            total = total + jnp.where(hit, 1.0, 0.0)
        return total

    def gather_near(reader, window, slot, dims):
        near[reader] += amount(reader, window) * mul(vhl[window], kh[slot], kl[slot], dims)

    near[...] = jnp.zeros_like(near)
    for leaf in range(LEAVES):
        columns_of(4 + leaf, ppad[:, leaf * LEAF : (leaf + 1) * LEAF])

    def spread(pair, slot):
        first, second = pair
        gather_near(first, 4 + second, slot, NORMAL)
        if first != second:
            gather_near(second, 4 + first, slot, TRANSPOSED)

    def local_pairs(pairs):
        for place in range(len(pairs) + 1):
            if place < len(pairs):
                first, second = pairs[place]
                evaluate(first, 4 + second, place % 2)
            if place > 0:
                spread(pairs[place - 1], (place - 1) % 2)

    every = [(a, b) for a in range(LEAVES) for b in range(a, LEAVES)]
    local_pairs(every[:LOCAL_FIRST])

    copy(sa.at[pl.ds(0, PLANE - 1)], e2.at[pl.ds(HALO, PLANE - 1)], SEM_A, left).wait_recv()
    edge_copies = []

    def send_edges(level):
        ref, nodes = edge_of[level], nodes_at(level)
        width = min(HALO, nodes)
        at = SEM_EDGE + 2 * (level - 2)
        for item in (
            copy(
                ref.at[pl.ds(HALO + nodes - width, width)],
                ref.at[pl.ds(HALO - width, width)],
                at,
                above,
            ),
            copy(ref.at[pl.ds(HALO, width)], ref.at[pl.ds(HALO + nodes, width)], at + 1, below),
        ):
            item.start()
            edge_copies.append(item)

    send_edges(2)
    for item in side_copies[:4]:
        item.start()
    for p in range(PLANE):
        g2[ROWS * p : ROWS * (p + 1), :] = e2[HALO + reversed_bits(p, 5), :, 0:RANK]
    current = g2[...]
    for level in (3, 4, 5, 6, 7):
        rows = ROWS * nodes_at(level)
        both = jnp.concatenate([current[: max(rows, 8)], second_half(current, rows)], axis=1)
        current = parents(both)
        if level < 7:
            count = 7 - level
            for p in range(nodes_at(level)):
                edge_of[level][HALO + reversed_bits(p, count)] = current[ROWS * p : ROWS * (p + 1)]
            if level - 3 < LOCAL_CHAIN:
                pair = every[LOCAL_FIRST + level - 3]
                evaluate(pair[0], 4 + pair[1], level % 2)
                spread(pair, level % 2)
    s7[...] = current[0:ROWS]

    for step in COLUMN_ORDER:
        copy(s7, top7.at[HALO + z], SEM_TOP, in_column(step) * PLANE + j).start()
    for level in PLANE_LEVELS[1:]:
        send_edges(level)
    for item in side_copies[4:]:
        item.start()
    middle = every[LOCAL_FIRST + LOCAL_CHAIN :]
    local_pairs(middle)

    top7[HALO + z] = s7[...]

    inside_below = jnp.where(z > 0, 1.0, 0.0)
    inside_above = jnp.where(z < PLANES - 1, 1.0, 0.0)

    def plane_field(level):
        ref, nodes = edge_of[level], nodes_at(level)
        count, slot = 7 - level, level - 2

        def at(node):
            value = ref[HALO + node, :, 0:RANK]
            if node < 0:
                value = value * inside_below
            if node >= nodes:
                value = value * inside_above
            return value

        for p in range(nodes):
            node = reversed_bits(p, count)
            rows = slice(ROWS * p, ROWS * (p + 1))
            gm[slot, rows, :] = at(node - 2)
            gp[slot, rows, :] = at(node + 2)
            if p < nodes // 2:
                ge[slot, rows, :] = at(node + 3)
            else:
                half = p - nodes // 2
                go[slot, ROWS * half : ROWS * (half + 1), :] = at(node - 3)
            if level == 2:
                gf[rows, :] = ref[HALO + node, :, RANK : RANK + 8]
        size = max(ROWS * nodes, 8)
        half_size = max(ROWS * nodes // 2, 8)
        minus, plus = gm[slot, 0:size, :], gp[slot, 0:size, :]
        even, odd = ge[slot, 0:half_size, :], go[slot, 0:half_size, :]
        if level == 2:
            weights = gf[0:size, :]
            minus = minus * weights[:, 0:1]
            plus = plus * weights[:, 1:2]
            even = even * weights[:half_size, 2:3]
            odd = odd * weights[half_size:, 2:3]
        fs[level - 2, 0:size, :] = field(level, minus, plus, even, odd, ROWS * nodes // 2)

    for item in edge_copies[:2]:
        item.wait_recv()
    plane_field(2)
    for item in edge_copies[2:]:
        item.wait_recv()
    for level in PLANE_LEVELS[1:]:
        plane_field(level)

    def take_sides(items, side_leaves):
        for item in items:
            item.wait_recv()
        for side, leaf in side_leaves:
            lanes = slice(leaf * LEAF, (leaf + 1) * LEAF)
            vhl[8 * side + leaf] = halves(vside[side, :, lanes])
            columns_of(8 * side + leaf, pside[side, :, lanes])

    def place_of(index):
        if isinstance(index, int):
            return (index // 2, 3 - index % 2) if index < 7 else (3 - (index - 7) // 2, 8 + (index - 7) % 2)
        on_left = index < 7
        place = jnp.where(on_left, index, index - 7)
        half, odd = lax.div(place, 2), lax.rem(place, 2)
        return jnp.where(on_left, half, 3 - half), jnp.where(on_left, 3 - odd, 8 + odd)

    def side_pairs(start, stop):
        evaluate(*place_of(start), 1)

        @pl.loop(0, (stop - start - 1) // 2)
        def _(step):
            index = start + 2 * step
            evaluate(*place_of(index + 1), 0)
            gather_near(*place_of(index), 1, NORMAL)
            evaluate(*place_of(index + 2), 1)
            gather_near(*place_of(index + 1), 0, NORMAL)

        if (stop - start) % 2 == 0:
            evaluate(*place_of(stop - 1), 0)
            gather_near(*place_of(stop - 2), 1, NORMAL)
            gather_near(*place_of(stop - 1), 0, NORMAL)
        else:
            gather_near(*place_of(stop - 1), 1, NORMAL)


    copy(
        top7.at[pl.ds(HALO, PLANES - 1)], top7.at[pl.ds(HALO, PLANES - 1)], SEM_TOP, left
    ).wait_recv()
    for p in range(PLANES):
        g2[ROWS * p : ROWS * (p + 1), :] = top7[HALO + reversed_bits(p, 3)]
    coef8 = parents(jnp.concatenate([g2[0:8, :], g2[8:16, :]], axis=1))
    for p in range(4):
        top8[HALO + reversed_bits(p, 2)] = coef8[ROWS * p : ROWS * (p + 1)]

    def own_field(level, ref, node):
        parity = node % 2
        slot = level - 2
        gm[slot, 0:ROWS, :] = ref[HALO + node - 2]
        gp[slot, 0:ROWS, :] = ref[HALO + node + 2]
        ge[slot, 0:ROWS, :] = ref[jnp.where(parity == 0, HALO + node + 3, HALO + node - 3)]
        third = ge[slot, 0:8, :]
        minus, plus = gm[slot, 0:8, :], gp[slot, 0:8, :]
        first, second, even, odd = field(level, minus, plus, third, third, None)
        return (first + second + jnp.where(parity == 0, even, odd)) * (1.0 / 32.0)

    def children(parent):
        return mul(halves(parent), th[...], tl[...], TRANSPOSED)

    field7 = own_field(7, top7, z)
    down = own_field(8, top8, z // 2)
    both = children(down)
    down = field7 + jnp.where(z % 2 == 0, both[:, :RANK], both[:, RANK:])
    take_sides(side_copies[:4], ((0, 2), (0, 3), (1, 0), (1, 1)))
    for level in (6, 5, 4, 3, 2):
        size = max(ROWS * nodes_at(level), 8)
        both = children(down)
        rows = ROWS * nodes_at(level) // 2
        down = fs[level - 2, 0:size, :] + stack(both[:, :RANK], both[:, RANK:], rows)
        for pair in CHAIN_PAIRS[6 - level]:
            evaluate(*place_of(pair), pair % 2)
            gather_near(*place_of(pair), pair % 2, NORMAL)
    for p in range(PLANE):
        sb[reversed_bits(p, 5)] = down[ROWS * p : ROWS * (p + 1)]

    for step in PLANE_ORDER:
        other = in_plane(step)
        copy(sb.at[other], rb.at[j], SEM_B, z * PLANE + other).start()

    rb[j] = sb[j]

    side_pairs(sum(len(group) for group in CHAIN_PAIRS), 14)
    take_sides(side_copies[4:6], ((0, 0), (0, 1), (1, 2), (1, 3)))
    for item in side_copies[6:]:
        item.wait_recv()
    has_left = jnp.where(me > 0, 1.0, 0.0)
    has_right = jnp.where(me < DEVICES - 1, 1.0, 0.0)

    def local_field(level, ref, nodes, first_row, target):
        def at(node, which, reader):
            weight = flags[which, first_row + reader].astype(F32)
            if node < 0:
                weight = weight * has_left
            if node >= nodes:
                weight = weight * has_right
            return ref[2 + node] * weight

        order = list(range(0, nodes, 2)) + list(range(1, nodes, 2))
        minus = jnp.concatenate([at(n - 2, 0, n) for n in order], axis=0)
        plus = jnp.concatenate([at(n + 2, 1, n) for n in order], axis=0)
        even = jnp.concatenate([at(n + 3, 2, n) for n in range(0, nodes, 2)], axis=0)
        odd = jnp.concatenate([at(n - 3, 2, n) for n in range(1, nodes, 2)], axis=0)
        value = field(level, minus, plus, even, odd, RHS * nodes // 2)
        for place, n in enumerate(order):
            target[n] = value[RHS * place : RHS * (place + 1)]

    last = ((0, 0), (0, 1), (1, 1), (3, 11), (3, 10), (2, 10))
    for item in range(len(last) + 1):
        if item < len(last):
            evaluate(*last[item], item % 2)
        if item == 0:
            local_field(0, ex0, LEAVES, 0, f0)
        if item == 1:
            local_field(1, ex1, LEAVES // 2, LEAVES, f1)
        if item > 0:
            gather_near(*last[item - 1], (item - 1) % 2, NORMAL)

    copy(sb.at[pl.ds(0, PLANE - 1)], rb.at[pl.ds(0, PLANE - 1)], SEM_B, left).wait_recv()
    for i in range(PLANE):
        g2[ROWS * i : ROWS * (i + 1), :] = rb[i]
    both = children(g2[...])
    down1 = jnp.concatenate([f1[0] + both[:, :RANK], f1[1] + both[:, RANK:]], axis=0)
    both = children(down1)
    for leaf in range(LEAVES):
        lanes = slice(leaf * LEAF, (leaf + 1) * LEAF)
        part = both[RHS * (leaf // 2) : RHS * (leaf // 2 + 1)]
        part = part[:, RANK * (leaf % 2) : RANK * (leaf % 2 + 1)]
        far = mul(halves(f0[leaf] + part), bh[:, lanes], bl[:, lanes])
        own = noise[:, lanes] * vec[:, lanes]
        out[:, lanes] = own + far + near[leaf] * (1.0 / 32.0)

    copy(sa.at[pl.ds(0, PLANE - 1)], e2.at[pl.ds(HALO, PLANE - 1)], SEM_A, left).wait_send()
    copy(sb.at[pl.ds(0, PLANE - 1)], rb.at[pl.ds(0, PLANE - 1)], SEM_B, left).wait_send()
    copy(
        top7.at[pl.ds(HALO, PLANES - 1)], top7.at[pl.ds(HALO, PLANES - 1)], SEM_TOP, left
    ).wait_send()
    for item in side_copies + edge_copies:
        item.wait_send()


def on_device(vectors, points, noise, bases, transfer, proxies, near_src, near_count, far_flags):
    vmem = pl.BlockSpec(memory_space=pltpu.VMEM)
    width = RANK + 128

    def buffer(*shape, dtype=F32):
        return pltpu.VMEM(shape, dtype)

    points_count = LEAVES * LEAF
    scratch = [
        buffer(RHS, points_count),
        buffer(3, points_count),
        buffer(1, points_count),
        buffer(RANK, points_count),
        buffer(2, RANK, RANK),
        buffer(3, RANK),
        pltpu.SMEM((LEAVES, 8), jnp.int32),
        pltpu.SMEM((LEAVES,), jnp.int32),
        pltpu.SMEM((3, 2 * LEAVES - 1), jnp.int32),
        buffer(12, 2 * RHS, LEAF, dtype=BF16),
        buffer(RANK, LEAVES * LEAF, dtype=BF16),
        buffer(RANK, LEAVES * LEAF, dtype=BF16),
        buffer(2 * RANK, RANK, dtype=BF16),
        buffer(2 * RANK, RANK, dtype=BF16),
        buffer(2, RHS, LEAVES * LEAF),
        buffer(8, LEAVES * LEAF),
        buffer(2, 8, LEAVES * LEAF),
        buffer(12, LEAF, 8),
        buffer(2, LEAF, LEAF, dtype=BF16),
        buffer(2, LEAF, LEAF, dtype=BF16),
        buffer(18, RANK, RANK, dtype=BF16),
        buffer(18, RANK, RANK, dtype=BF16),
        buffer(LEAVES, RHS, LEAF),
        buffer(LEAVES + 4, RHS, RANK),
        buffer(LEAVES // 2 + 4, RHS, RANK),
        buffer(LEAVES, RHS, RANK),
        buffer(LEAVES // 2, RHS, RANK),
        buffer(PLANE, ROWS, width),
        buffer(PLANE, ROWS, RANK),
        buffer(PLANE, ROWS, RANK),
        buffer(ROWS, RANK),
        buffer(PLANE + 2 * HALO, ROWS, width),
    ]
    for level in PLANE_LEVELS[1:]:
        scratch.append(buffer(nodes_at(level) + 2 * HALO, ROWS, RANK))
    scratch += [
        buffer(PLANES + 2 * HALO, ROWS, RANK),
        buffer(4 + 2 * HALO, ROWS, RANK),
        buffer(7, RHS, RANK),
        buffer(7, RHS, RANK),
        buffer(7, RHS, RANK),
        buffer(7, RHS, RANK),
        buffer(RANK, 8),
        buffer(RHS, RANK),
        buffer(len(PLANE_LEVELS), RHS, RANK),
        pltpu.SemaphoreType.DMA((9,)),
        pltpu.SemaphoreType.DMA((SEMS,)),
        pltpu.SemaphoreType.DMA((SEMS,)),
    ]
    return pl.pallas_call(
        kernel,
        out_shape=jax.ShapeDtypeStruct(vectors.shape, F32),
        in_specs=[pl.BlockSpec(memory_space=pltpu.HBM)] * 9,
        out_specs=vmem,
        scratch_shapes=scratch,
        compiler_params=pltpu.CompilerParams(
            collective_id=0, has_side_effects=True, vmem_limit_bytes=62 * 2**20
        ),
        cost_estimate=pl.CostEstimate(
            flops=3 * 10**9, bytes_accessed=3 * 10**6, transcendentals=10**7
        ),
    )(
        vectors,
        points,
        noise.reshape(1, -1),
        bases,
        transfer,
        proxies,
        near_src,
        near_count,
        far_flags.T,
    )


def solution(mesh):
    in_specs = (
        P(None, "leaf"),
        P(None, "leaf"),
        P("leaf"),
        P(None, "leaf"),
        P(),
        P(),
        P("leaf", None),
        P("leaf"),
        P("leaf", None),
    )
    return jax.shard_map(
        on_device, mesh=mesh, in_specs=in_specs, out_specs=P(None, "leaf"), check_vma=False
    )
```

```python
import jax
import jax.numpy as jnp
from jax import lax
from jax.experimental import pallas as pl
from jax.experimental.pallas import tpu as pltpu
from jax.sharding import PartitionSpec as P

SHORT_SCALE = 0.02
LONG_SCALE = 1.0
ROOT_THREE = 1.7320508075688772
LOG2_E = 1.4426950408889634

F32 = jnp.float32
BF16 = jnp.bfloat16
MESH = pl.DeviceIdType.MESH

LEAVES = 4
LEAF = 256
RANK = 256
RHS = 64
ROWS = 2
PLANE = 32
PLANES = 8
DEVICES = PLANE * PLANES
TOP = 10
HALO = 3
CHUNK = 32
LOCAL_FIRST = 4
LOCAL_CHAIN = 4
CHAIN_PAIRS = ((0,), (1,), (2,), (3,), (4,))

NORMAL = (((1,), (0,)), ((), ()))
TRANSPOSED = (((1,), (1,)), ((), ()))

PLANE_LEVELS = (2, 3, 4, 5, 6)

PLANE_ORDER = sorted(
    range(1, PLANE), key=lambda s: -(min(s // 8, 4 - s // 8) + min(s // 2 % 4, 4 - s // 2 % 4))
)
COLUMN_ORDER = (4, 3, 5, 2, 6, 1, 7)

SEM_A, SEM_TOP, SEM_B = 0, 1, 2
SEM_VEC, SEM_PTS, SEM_RIM0, SEM_RIM1, SEM_FAR, SEM_EDGE = 3, 5, 7, 9, 11, 13
SEMS = SEM_EDGE + 2 * len(PLANE_LEVELS)


def nodes_at(level):
    return PLANE >> (level - 2)


def reversed_bits(value, count):
    result = 0
    for bit in range(count):
        result = result * 2 + (value >> bit & 1)
    return result


def halves(x):
    head = x.astype(BF16).astype(F32)
    return jnp.concatenate([head, x - head], axis=0).astype(BF16)


def head_and_rest(x):
    head = x.astype(BF16)
    return head, (x - head.astype(F32)).astype(BF16)


def mul(stacked, w_head, w_rest, dims=NORMAL):
    rows = stacked.shape[0] // 2
    if rows % 16 == 0:
        first = lax.dot_general(stacked, w_head, dims, preferred_element_type=F32)
        second = lax.dot_general(stacked[:rows], w_rest, dims, preferred_element_type=F32)
        return first[:rows] + first[rows:] + second
    both = lax.dot_general(stacked, w_head, dims, preferred_element_type=F32)
    both = both + lax.dot_general(stacked, w_rest, dims, preferred_element_type=F32)
    return both[:rows] + both[rows:]


def stack(first, second, rows):
    if rows % 8 == 0:
        return jnp.concatenate([first[:rows], second[:rows]], axis=0)
    place = lax.broadcasted_iota(jnp.int32, first.shape, 0)
    return jnp.where(place < rows, first, pltpu.roll(second, rows, 0))


def second_half(x, rows):
    if rows % 8 == 0:
        return x[rows:]
    return pltpu.roll(x, x.shape[0] - rows, 0)


def kernel(
    vec_in,
    pts_in,
    noise_in,
    bases_in,
    transfer_in,
    prox_in,
    src_in,
    cnt_in,
    flags_in,
    out,
    result,
    store,
    vec,
    pts,
    noise,
    bases,
    transfer,
    prox,
    src,
    cnt,
    flags,
    vhl,
    bh,
    bl,
    th,
    tl,
    vside,
    ppad,
    pside,
    cols,
    kh,
    kl,
    ch,
    cl,
    near,
    ex0,
    ex1,
    f0,
    f1,
    sa,
    sb,
    rb,
    s7,
    e2,
    e3,
    e4,
    e5,
    e6,
    top7,
    top8,
    gm,
    gp,
    ge,
    go,
    gf,
    g2,
    fs,
    load,
    send,
    recv,
):
    loads = [
        pltpu.make_async_copy(source, target, load.at[place])
        for place, (source, target) in enumerate(
            (
                (vec_in, vec),
                (bases_in, bases),
                (transfer_in, transfer),
                (pts_in, pts),
                (prox_in, prox),
                (noise_in, noise),
                (src_in, src),
                (cnt_in, cnt),
                (flags_in, flags),
            )
        )
    ]
    edge_of = {2: e2, 3: e3, 4: e4, 5: e5, 6: e6}
    me = lax.axis_index("leaf")
    z, j = me // PLANE, me % PLANE
    left = (me + DEVICES - 1) % DEVICES
    right = (me + 1) % DEVICES
    below = (me + DEVICES - PLANE) % DEVICES
    above = (me + PLANE) % DEVICES

    barrier = pltpu.get_barrier_semaphore()

    def greet(device):
        pl.semaphore_signal(barrier, inc=1, device_id=(device,), device_id_type=MESH)

    def in_plane(step):
        return lax.rem(j + step, PLANE)

    def in_column(step):
        return lax.rem(z + step, PLANES)

    for step in PLANE_ORDER:
        greet(z * PLANE + in_plane(step))
    for step in COLUMN_ORDER:
        greet(in_column(step) * PLANE + j)
    greet(left)
    greet(right)
    for item in loads:
        item.start()

    def copy(source, target, sem, device):
        return pltpu.make_async_remote_copy(
            src_ref=source,
            dst_ref=target,
            send_sem=send.at[sem],
            recv_sem=recv.at[sem],
            device_id=(device,),
            device_id_type=MESH,
        )

    for item in loads:
        item.wait()
    head, rest = head_and_rest(transfer[...].reshape(2 * RANK, RANK))
    th[...] = head
    tl[...] = rest
    coef0 = []
    for leaf in range(LEAVES):
        lanes = slice(leaf * LEAF, (leaf + 1) * LEAF)
        head, rest = head_and_rest(bases[:, lanes])
        bh[:, lanes] = head
        bl[:, lanes] = rest
        pair = halves(vec[:, lanes])
        vhl[4 + leaf] = pair
        value = mul(pair, head, rest, TRANSPOSED)
        ex0[2 + leaf] = value
        coef0.append(value)

    def parents(children):
        return mul(halves(children), th[...], tl[...])

    pair_rows = [jnp.concatenate([coef0[2 * n], coef0[2 * n + 1]], axis=1) for n in range(2)]
    coef1 = parents(jnp.concatenate(pair_rows, axis=0))
    ex1[2] = coef1[:RHS]
    ex1[3] = coef1[RHS:]
    coef2 = parents(jnp.concatenate([coef1[:RHS], coef1[RHS:]], axis=1))

    lane = lax.broadcasted_iota(jnp.int32, (ROWS, 128), 1)
    root_flags = jnp.zeros((ROWS, 128), F32)
    for which in range(3):
        root_flags = jnp.where(lane == which, flags[which, 6].astype(F32), root_flags)
    g2[...] = coef2
    for i in range(PLANE):
        sa[i, :, 0:RANK] = g2[ROWS * i : ROWS * (i + 1), :]
        sa[i, :, RANK:] = root_flags

    pl.semaphore_wait(barrier, PLANE - 1 + PLANES - 1 + 2)

    for step in PLANE_ORDER:
        other = in_plane(step)
        copy(sa.at[other], e2.at[HALO + j], SEM_A, z * PLANE + other).start()

    e2[HALO + j] = sa[j]

    ppad[...] = jnp.zeros_like(ppad)
    ppad[0:3, :] = pts[...]

    def side_copy(side, first, sem, device):
        lanes = pl.ds(first * LEAF, 2 * LEAF)
        return copy(vec.at[:, lanes], vside.at[side, :, lanes], sem, device)

    side_copies = [
        copy(ppad, pside.at[0], SEM_PTS, right),
        copy(ppad, pside.at[1], SEM_PTS + 1, left),
        side_copy(0, 2, SEM_VEC, right),
        side_copy(1, 0, SEM_VEC + 1, left),
        side_copy(0, 0, SEM_FAR, right),
        side_copy(1, 2, SEM_FAR + 1, left),
        copy(ex0.at[pl.ds(4, 2)], ex0.at[pl.ds(0, 2)], SEM_RIM0, right),
        copy(ex0.at[pl.ds(2, 2)], ex0.at[pl.ds(6, 2)], SEM_RIM0 + 1, left),
        copy(ex1.at[pl.ds(2, 2)], ex1.at[pl.ds(0, 2)], SEM_RIM1, right),
        copy(ex1.at[pl.ds(2, 2)], ex1.at[pl.ds(4, 2)], SEM_RIM1 + 1, left),
    ]
    prox_rows = prox[...]
    prox_cols = jnp.concatenate([prox_rows, jnp.zeros((5, RANK), F32)], axis=0).T
    gf[...] = prox_cols

    for axis in range(3):
        side = 2.0 ** ((axis - TOP) / 3.0)
        for place, offset in enumerate((2.0, 3.0)):
            for step in range(RANK // CHUNK):
                rows = slice(step * CHUNK, (step + 1) * CHUNK)
                squared = None
                for c in range(3):
                    column = gf[rows, c : c + 1]
                    if c == axis:
                        column = column - offset
                    delta = column - prox_rows[c : c + 1, :]
                    squared = delta * delta if squared is None else squared + delta * delta
                distance = squared * lax.rsqrt(jnp.maximum(squared, 1e-30))
                u = distance * (ROOT_THREE / SHORT_SCALE * side)
                v = distance * (ROOT_THREE / LONG_SCALE * side)
                eu = jnp.exp2(u * -LOG2_E)
                ev = jnp.exp2(v * -LOG2_E)
                for third in range(3):
                    value = (1.0 + u) * eu + (1.0 + v) * ev
                    head, rest = head_and_rest(value)
                    at = 2 * (axis + 3 * third) + place
                    ch[at, rows, :] = head
                    cl[at, rows, :] = rest
                    if third < 2:
                        u, v, eu, ev = u + u, v + v, eu * eu, ev * ev

    def field(level, minus, plus, even, odd, rows):
        two, three = 2 * level, 2 * level + 1
        first = mul(halves(minus), ch[two], cl[two])
        second = mul(halves(plus), ch[two], cl[two], TRANSPOSED)
        even_part = mul(halves(even), ch[three], cl[three], TRANSPOSED)
        odd_part = mul(halves(odd), ch[three], cl[three])
        if rows is None:
            return first, second, even_part, odd_part
        return (first + second + stack(even_part, odd_part, rows)) * (1.0 / 32.0)

    top7[0:HALO] = jnp.zeros((HALO, ROWS, RANK), F32)
    top7[HALO + PLANES :] = jnp.zeros((HALO, ROWS, RANK), F32)
    top8[...] = jnp.zeros_like(top8)
    gm[...] = jnp.zeros_like(gm)
    gp[...] = jnp.zeros_like(gp)
    ge[...] = jnp.zeros_like(ge)
    go[...] = jnp.zeros_like(go)

    def columns_of(window, points):
        cols[window] = points.T

    def evaluate(reader, window, slot):
        reader_rows = ppad[:, pl.ds(pl.multiple_of(reader * LEAF, LEAF), LEAF)]
        for step in range(LEAF // CHUNK):
            rows = slice(step * CHUNK, (step + 1) * CHUNK)
            squared = None
            for c in range(3):
                delta = cols[window, rows, c : c + 1] - reader_rows[c : c + 1, :]
                squared = delta * delta if squared is None else squared + delta * delta
            distance = squared * lax.rsqrt(jnp.maximum(squared, 1e-30))
            short, long = ROOT_THREE / SHORT_SCALE, ROOT_THREE / LONG_SCALE
            value = (1.0 + distance * short) * jnp.exp2(distance * (-LOG2_E * short))
            value = value + (1.0 + distance * long) * jnp.exp2(distance * (-LOG2_E * long))
            head, rest = head_and_rest(value)
            kh[slot, rows, :] = head
            kl[slot, rows, :] = rest

    def amount(reader, window):
        target = me * LEAVES + window - 4
        total = jnp.float32(0.0)
        for slot in range(8):
            hit = jnp.logical_and(slot < cnt[reader], src[reader, slot] == target)
            total = total + jnp.where(hit, 1.0, 0.0)
        return total

    def gather_near(reader, window, slot, dims):
        near[reader] += amount(reader, window) * mul(vhl[window], kh[slot], kl[slot], dims)

    near[...] = jnp.zeros_like(near)
    for leaf in range(LEAVES):
        columns_of(4 + leaf, ppad[:, leaf * LEAF : (leaf + 1) * LEAF])

    def spread(pair, slot):
        first, second = pair
        gather_near(first, 4 + second, slot, NORMAL)
        if first != second:
            gather_near(second, 4 + first, slot, TRANSPOSED)

    def local_pairs(pairs):
        for place in range(len(pairs) + 1):
            if place < len(pairs):
                first, second = pairs[place]
                evaluate(first, 4 + second, place % 2)
            if place > 0:
                spread(pairs[place - 1], (place - 1) % 2)

    every = [(a, b) for a in range(LEAVES) for b in range(a, LEAVES)]
    local_pairs(every[:LOCAL_FIRST])

    copy(sa.at[pl.ds(0, PLANE - 1)], e2.at[pl.ds(HALO, PLANE - 1)], SEM_A, left).wait_recv()
    edge_copies = []

    def send_edges(level):
        ref, nodes = edge_of[level], nodes_at(level)
        width = min(HALO, nodes)
        at = SEM_EDGE + 2 * (level - 2)
        for item in (
            copy(
                ref.at[pl.ds(HALO + nodes - width, width)],
                ref.at[pl.ds(HALO - width, width)],
                at,
                above,
            ),
            copy(ref.at[pl.ds(HALO, width)], ref.at[pl.ds(HALO + nodes, width)], at + 1, below),
        ):
            item.start()
            edge_copies.append(item)

    send_edges(2)
    for item in side_copies[:4]:
        item.start()
    for p in range(PLANE):
        g2[ROWS * p : ROWS * (p + 1), :] = e2[HALO + reversed_bits(p, 5), :, 0:RANK]
    current = g2[...]
    for level in (3, 4, 5, 6, 7):
        rows = ROWS * nodes_at(level)
        both = jnp.concatenate([current[: max(rows, 8)], second_half(current, rows)], axis=1)
        current = parents(both)
        if level < 7:
            count = 7 - level
            for p in range(nodes_at(level)):
                edge_of[level][HALO + reversed_bits(p, count)] = current[ROWS * p : ROWS * (p + 1)]
            if level - 3 < LOCAL_CHAIN:
                pair = every[LOCAL_FIRST + level - 3]
                evaluate(pair[0], 4 + pair[1], level % 2)
                spread(pair, level % 2)
    s7[...] = current[0:ROWS]

    for step in COLUMN_ORDER:
        copy(s7, top7.at[HALO + z], SEM_TOP, in_column(step) * PLANE + j).start()
    for level in PLANE_LEVELS[1:]:
        send_edges(level)
    for item in side_copies[4:]:
        item.start()
    middle = every[LOCAL_FIRST + LOCAL_CHAIN :]
    local_pairs(middle)

    top7[HALO + z] = s7[...]

    inside_below = jnp.where(z > 0, 1.0, 0.0)
    inside_above = jnp.where(z < PLANES - 1, 1.0, 0.0)

    def plane_field(level):
        ref, nodes = edge_of[level], nodes_at(level)
        count, slot = 7 - level, level - 2

        def at(node):
            value = ref[HALO + node, :, 0:RANK]
            if node < 0:
                value = value * inside_below
            if node >= nodes:
                value = value * inside_above
            return value

        for p in range(nodes):
            node = reversed_bits(p, count)
            rows = slice(ROWS * p, ROWS * (p + 1))
            gm[slot, rows, :] = at(node - 2)
            gp[slot, rows, :] = at(node + 2)
            if p < nodes // 2:
                ge[slot, rows, :] = at(node + 3)
            else:
                half = p - nodes // 2
                go[slot, ROWS * half : ROWS * (half + 1), :] = at(node - 3)
            if level == 2:
                gf[rows, :] = ref[HALO + node, :, RANK : RANK + 8]
        size = max(ROWS * nodes, 8)
        half_size = max(ROWS * nodes // 2, 8)
        minus, plus = gm[slot, 0:size, :], gp[slot, 0:size, :]
        even, odd = ge[slot, 0:half_size, :], go[slot, 0:half_size, :]
        if level == 2:
            weights = gf[0:size, :]
            minus = minus * weights[:, 0:1]
            plus = plus * weights[:, 1:2]
            even = even * weights[:half_size, 2:3]
            odd = odd * weights[half_size:, 2:3]
        fs[level - 2, 0:size, :] = field(level, minus, plus, even, odd, ROWS * nodes // 2)

    for item in edge_copies[:2]:
        item.wait_recv()
    plane_field(2)
    for item in edge_copies[2:]:
        item.wait_recv()
    for level in PLANE_LEVELS[1:]:
        plane_field(level)

    def take_sides(items, side_leaves):
        for item in items:
            item.wait_recv()
        for side, leaf in side_leaves:
            lanes = slice(leaf * LEAF, (leaf + 1) * LEAF)
            vhl[8 * side + leaf] = halves(vside[side, :, lanes])
            columns_of(8 * side + leaf, pside[side, :, lanes])

    def place_of(index):
        if isinstance(index, int):
            return (index // 2, 3 - index % 2) if index < 7 else (3 - (index - 7) // 2, 8 + (index - 7) % 2)
        on_left = index < 7
        place = jnp.where(on_left, index, index - 7)
        half, odd = lax.div(place, 2), lax.rem(place, 2)
        return jnp.where(on_left, half, 3 - half), jnp.where(on_left, 3 - odd, 8 + odd)

    def side_pairs(start, stop):
        evaluate(*place_of(start), 1)

        @pl.loop(0, (stop - start - 1) // 2)
        def _(step):
            index = start + 2 * step
            evaluate(*place_of(index + 1), 0)
            gather_near(*place_of(index), 1, NORMAL)
            evaluate(*place_of(index + 2), 1)
            gather_near(*place_of(index + 1), 0, NORMAL)

        if (stop - start) % 2 == 0:
            evaluate(*place_of(stop - 1), 0)
            gather_near(*place_of(stop - 2), 1, NORMAL)
            gather_near(*place_of(stop - 1), 0, NORMAL)
        else:
            gather_near(*place_of(stop - 1), 1, NORMAL)


    copy(
        top7.at[pl.ds(HALO, PLANES - 1)], top7.at[pl.ds(HALO, PLANES - 1)], SEM_TOP, left
    ).wait_recv()
    for p in range(PLANES):
        g2[ROWS * p : ROWS * (p + 1), :] = top7[HALO + reversed_bits(p, 3)]
    coef8 = parents(jnp.concatenate([g2[0:8, :], g2[8:16, :]], axis=1))
    for p in range(4):
        top8[HALO + reversed_bits(p, 2)] = coef8[ROWS * p : ROWS * (p + 1)]

    def own_field(level, ref, node):
        parity = node % 2
        slot = level - 2
        gm[slot, 0:ROWS, :] = ref[HALO + node - 2]
        gp[slot, 0:ROWS, :] = ref[HALO + node + 2]
        ge[slot, 0:ROWS, :] = ref[jnp.where(parity == 0, HALO + node + 3, HALO + node - 3)]
        third = ge[slot, 0:8, :]
        minus, plus = gm[slot, 0:8, :], gp[slot, 0:8, :]
        first, second, even, odd = field(level, minus, plus, third, third, None)
        return (first + second + jnp.where(parity == 0, even, odd)) * (1.0 / 32.0)

    def children(parent):
        return mul(halves(parent), th[...], tl[...], TRANSPOSED)

    field7 = own_field(7, top7, z)
    down = own_field(8, top8, z // 2)
    both = children(down)
    down = field7 + jnp.where(z % 2 == 0, both[:, :RANK], both[:, RANK:])
    take_sides(side_copies[:4], ((0, 2), (0, 3), (1, 0), (1, 1)))
    for level in (6, 5, 4, 3, 2):
        size = max(ROWS * nodes_at(level), 8)
        both = children(down)
        rows = ROWS * nodes_at(level) // 2
        down = fs[level - 2, 0:size, :] + stack(both[:, :RANK], both[:, RANK:], rows)
        for pair in CHAIN_PAIRS[6 - level]:
            evaluate(*place_of(pair), pair % 2)
            gather_near(*place_of(pair), pair % 2, NORMAL)
    for p in range(PLANE):
        sb[reversed_bits(p, 5)] = down[ROWS * p : ROWS * (p + 1)]

    for step in PLANE_ORDER:
        other = in_plane(step)
        copy(sb.at[other], rb.at[j], SEM_B, z * PLANE + other).start()

    rb[j] = sb[j]

    side_pairs(sum(len(group) for group in CHAIN_PAIRS), 14)
    take_sides(side_copies[4:6], ((0, 0), (0, 1), (1, 2), (1, 3)))
    for item in side_copies[6:]:
        item.wait_recv()
    has_left = jnp.where(me > 0, 1.0, 0.0)
    has_right = jnp.where(me < DEVICES - 1, 1.0, 0.0)

    def local_field(level, ref, nodes, first_row, target):
        def at(node, which, reader):
            weight = flags[which, first_row + reader].astype(F32)
            if node < 0:
                weight = weight * has_left
            if node >= nodes:
                weight = weight * has_right
            return ref[2 + node] * weight

        order = list(range(0, nodes, 2)) + list(range(1, nodes, 2))
        minus = jnp.concatenate([at(n - 2, 0, n) for n in order], axis=0)
        plus = jnp.concatenate([at(n + 2, 1, n) for n in order], axis=0)
        even = jnp.concatenate([at(n + 3, 2, n) for n in range(0, nodes, 2)], axis=0)
        odd = jnp.concatenate([at(n - 3, 2, n) for n in range(1, nodes, 2)], axis=0)
        value = field(level, minus, plus, even, odd, RHS * nodes // 2)
        for place, n in enumerate(order):
            target[n] = value[RHS * place : RHS * (place + 1)]

    last = ((0, 0), (0, 1), (1, 1), (3, 11), (3, 10), (2, 10))
    for item in range(len(last) + 1):
        if item < len(last):
            evaluate(*last[item], item % 2)
        if item == 0:
            local_field(0, ex0, LEAVES, 0, f0)
        if item == 1:
            local_field(1, ex1, LEAVES // 2, LEAVES, f1)
        if item > 0:
            gather_near(*last[item - 1], (item - 1) % 2, NORMAL)

    copy(sb.at[pl.ds(0, PLANE - 1)], rb.at[pl.ds(0, PLANE - 1)], SEM_B, left).wait_recv()
    for i in range(PLANE):
        g2[ROWS * i : ROWS * (i + 1), :] = rb[i]
    both = children(g2[...])
    down1 = jnp.concatenate([f1[0] + both[:, :RANK], f1[1] + both[:, RANK:]], axis=0)
    both = children(down1)
    stores = []
    for leaf in range(LEAVES):
        lanes = slice(leaf * LEAF, (leaf + 1) * LEAF)
        part = both[RHS * (leaf // 2) : RHS * (leaf // 2 + 1)]
        part = part[:, RANK * (leaf % 2) : RANK * (leaf % 2 + 1)]
        far = mul(halves(f0[leaf] + part), bh[:, lanes], bl[:, lanes])
        own = noise[:, lanes] * vec[:, lanes]
        result[:, lanes] = own + far + near[leaf] * (1.0 / 32.0)
        stores.append(
            pltpu.make_async_copy(
                result.at[:, pl.ds(leaf * LEAF, LEAF)],
                out.at[:, pl.ds(leaf * LEAF, LEAF)],
                store.at[leaf],
            )
        )
        stores[-1].start()

    for item in stores:
        item.wait()
    copy(sa.at[pl.ds(0, PLANE - 1)], e2.at[pl.ds(HALO, PLANE - 1)], SEM_A, left).wait_send()
    copy(sb.at[pl.ds(0, PLANE - 1)], rb.at[pl.ds(0, PLANE - 1)], SEM_B, left).wait_send()
    copy(
        top7.at[pl.ds(HALO, PLANES - 1)], top7.at[pl.ds(HALO, PLANES - 1)], SEM_TOP, left
    ).wait_send()
    for item in side_copies + edge_copies:
        item.wait_send()


def on_device(vectors, points, noise, bases, transfer, proxies, near_src, near_count, far_flags):
    width = RANK + 128

    def buffer(*shape, dtype=F32):
        return pltpu.VMEM(shape, dtype)

    points_count = LEAVES * LEAF
    scratch = [
        buffer(RHS, points_count),
        pltpu.SemaphoreType.DMA((LEAVES,)),
        buffer(RHS, points_count),
        buffer(3, points_count),
        buffer(1, points_count),
        buffer(RANK, points_count),
        buffer(2, RANK, RANK),
        buffer(3, RANK),
        pltpu.SMEM((LEAVES, 8), jnp.int32),
        pltpu.SMEM((LEAVES,), jnp.int32),
        pltpu.SMEM((3, 2 * LEAVES - 1), jnp.int32),
        buffer(12, 2 * RHS, LEAF, dtype=BF16),
        buffer(RANK, LEAVES * LEAF, dtype=BF16),
        buffer(RANK, LEAVES * LEAF, dtype=BF16),
        buffer(2 * RANK, RANK, dtype=BF16),
        buffer(2 * RANK, RANK, dtype=BF16),
        buffer(2, RHS, LEAVES * LEAF),
        buffer(8, LEAVES * LEAF),
        buffer(2, 8, LEAVES * LEAF),
        buffer(12, LEAF, 8),
        buffer(2, LEAF, LEAF, dtype=BF16),
        buffer(2, LEAF, LEAF, dtype=BF16),
        buffer(18, RANK, RANK, dtype=BF16),
        buffer(18, RANK, RANK, dtype=BF16),
        buffer(LEAVES, RHS, LEAF),
        buffer(LEAVES + 4, RHS, RANK),
        buffer(LEAVES // 2 + 4, RHS, RANK),
        buffer(LEAVES, RHS, RANK),
        buffer(LEAVES // 2, RHS, RANK),
        buffer(PLANE, ROWS, width),
        buffer(PLANE, ROWS, RANK),
        buffer(PLANE, ROWS, RANK),
        buffer(ROWS, RANK),
        buffer(PLANE + 2 * HALO, ROWS, width),
    ]
    for level in PLANE_LEVELS[1:]:
        scratch.append(buffer(nodes_at(level) + 2 * HALO, ROWS, RANK))
    scratch += [
        buffer(PLANES + 2 * HALO, ROWS, RANK),
        buffer(4 + 2 * HALO, ROWS, RANK),
        buffer(7, RHS, RANK),
        buffer(7, RHS, RANK),
        buffer(7, RHS, RANK),
        buffer(7, RHS, RANK),
        buffer(RANK, 8),
        buffer(RHS, RANK),
        buffer(len(PLANE_LEVELS), RHS, RANK),
        pltpu.SemaphoreType.DMA((9,)),
        pltpu.SemaphoreType.DMA((SEMS,)),
        pltpu.SemaphoreType.DMA((SEMS,)),
    ]
    return pl.pallas_call(
        kernel,
        out_shape=jax.ShapeDtypeStruct(vectors.shape, F32),
        in_specs=[pl.BlockSpec(memory_space=pltpu.HBM)] * 9,
        out_specs=pl.BlockSpec(memory_space=pltpu.HBM),
        scratch_shapes=scratch,
        compiler_params=pltpu.CompilerParams(
            collective_id=0, has_side_effects=True, vmem_limit_bytes=62 * 2**20
        ),
        cost_estimate=pl.CostEstimate(
            flops=3 * 10**9, bytes_accessed=3 * 10**6, transcendentals=10**7
        ),
    )(
        vectors,
        points,
        noise.reshape(1, -1),
        bases,
        transfer,
        proxies,
        near_src,
        near_count,
        far_flags.T,
    )


def solution(mesh):
    in_specs = (
        P(None, "leaf"),
        P(None, "leaf"),
        P("leaf"),
        P(None, "leaf"),
        P(),
        P(),
        P("leaf", None),
        P("leaf"),
        P("leaf", None),
    )
    return jax.shard_map(
        on_device, mesh=mesh, in_specs=in_specs, out_specs=P(None, "leaf"), check_vma=False
    )
```
